512 devices in a mesh: wide: 32 (over y, x, core), narrow: 16 (over z).
Axes of the slice: x: 4, y: 4, z: 16, core: 2. Of those that a mesh axis runs over, the one named last changes fastest.
Arguments:
- factors: bfloat16 [32, 8192, 512], P('narrow', 'wide'), may hold values from -0.41992188 to 0.41992188
- pairs: int32 [256, 2], replicated, may hold values from 0 to 31, as said below
Outputs:
- exchange: float32 [8192, 8192], P(('wide', 'narrow'))
The draws below stay inside these ranges and needn't reach their ends.
Inputs may be any that keep to these rules, and one draw needn't show every extreme that they name: Rows are sorted by row block; each row block has 1 to 15 pairs and some row block exactly 15; column blocks within one row block are distinct.
All inputs are finite; a program needn't handle non-finite values.
Results may differ from the reference program's by a relative error of at most 0.0003.
Values may be sent and summed in bfloat16 or wider, within the bound.
A program may use at most 128 MiB of HBM per device.

```python
import jax
import jax.numpy as jnp
from jax import lax

ROWS_DEV = 256
OCC = 512
NBAS = 8192
AUX = 32
N_WIDE = 32


def draw_pairs(key, part):
    key = jax.random.fold_in(key, 11)
    nblk = N_WIDE
    mean_count = N_WIDE // 4
    first, second, third = jax.random.split(key, 3)
    order = jax.random.permutation(first, nblk)
    halves = jax.random.randint(second, (nblk // 2,), 0, mean_count)
    halves = halves.at[0].set(mean_count - 1)
    delta = jnp.zeros((nblk,), jnp.int32).at[order[0::2]].set(halves).at[order[1::2]].set(-halves)
    counts = mean_count + delta
    ends = jnp.cumsum(counts)
    starts = ends - counts
    index = jnp.arange(nblk * mean_count)
    row_block = jnp.sum((index[:, None] >= ends[None, :]).astype(jnp.int32), axis=1)
    position = index - starts[row_block]
    scores = jax.random.randint(third, (nblk, nblk), 0, 1 << 20) * nblk + jnp.arange(nblk)[None, :]
    shuffled = jnp.argsort(scores, axis=1, stable=True)
    col_block = shuffled[row_block, position]
    return jnp.stack([row_block, col_block], axis=1).astype(jnp.int32)


def block_levels(stream_key, dims, pieces, smallest, top_value):
    def one(dim, parts):
        heights = jax.random.uniform(jax.random.fold_in(jax.random.fold_in(stream_key, 6), dim), (parts,), jnp.float32, smallest / len(pieces), top_value / len(pieces))
        return jnp.repeat(jnp.exp(heights), dims[dim] // parts).reshape((-1,) + (1,) * (len(dims) - dim - 1))

    gain = one(*pieces[0])
    for cut in pieces[1:]:
        gain = gain * one(*cut)
    return gain


def scatter_about(rng, shape, scale, most, cuts=(), held_as=jnp.bfloat16):
    result = scale * jax.random.normal(rng, shape, jnp.float32)
    if cuts:
        result = result * block_levels(rng, shape, cuts, -0.22, 0.18)
    return jnp.clip(result, -most, most).astype(held_as)


def setup_inputs(seed: int = 0) -> dict:
    arg_keys = jax.random.split(jax.random.key(seed), 3)
    return {
        "factors": scatter_about(arg_keys[0], (AUX, NBAS, OCC), 0.07, 0.41992188, ((0, 16), (1, 32))),
        "pairs": draw_pairs(jax.random.fold_in(arg_keys[2], 71), 0),
    }


def reference(factors, pairs):
    nblk = NBAS // ROWS_DEV

    def one_tile(pair):
        left = lax.dynamic_slice_in_dim(factors, (pair[0] * ROWS_DEV).astype(jnp.int32), ROWS_DEV, 1)
        right = lax.dynamic_slice_in_dim(factors, (pair[1] * ROWS_DEV).astype(jnp.int32), ROWS_DEV, 1)
        return lax.dot_general(left, right, (((0, 2), (0, 2)), ((), ())), preferred_element_type=jnp.float32)

    tiles = lax.map(one_tile, pairs)
    blocks = jnp.zeros((nblk, ROWS_DEV, nblk, ROWS_DEV), jnp.float32)
    blocks = blocks.at[pairs[:, 0], :, pairs[:, 1], :].set(tiles)
    return blocks.reshape(NBAS, NBAS)
```

```python
import functools

import jax
import jax.numpy as jnp
from jax import lax
from jax.experimental import pallas as pl
from jax.experimental.pallas import tpu as pltpu
from jax.sharding import PartitionSpec as P

MESH = pl.DeviceIdType.MESH
NX = NY = 4
SLOTS = 16
STEP = 16.0
TOP = 32000.0


def place():
    w = lax.axis_index("wide")
    return w // (2 * NX), lax.rem(w // 2, NX), lax.rem(w, 2)


def wide(y, x, q):
    return {"wide": (y * NX + x) * 2 + q}


def item(axis, distance, other):
    if distance == 0:
        return other
    return (0 if axis == "x" else 2 * NX - 2) + 2 * distance + other


def cross_gather(buf, halves, axes, send, recv):
    y, x, q = place()
    near = {
        ("x", 1): wide(y, lax.rem(x + 1, NX), q),
        ("x", -1): wide(y, lax.rem(x + NX - 1, NX), q),
        ("y", 1): wide(lax.rem(y + 1, NY), x, q),
        ("y", -1): wide(lax.rem(y + NY - 1, NY), x, q),
        "core": wide(y, x, 1 - q),
    }
    started = []

    def copy(src, dst, half, to):
        c = pltpu.make_async_remote_copy(
            src_ref=buf.at[(src,) + halves[half]],
            dst_ref=buf.at[(dst,) + halves[half]],
            send_sem=send.at[len(started)],
            recv_sem=recv.at[dst, half],
            device_id=near[to],
            device_id_type=MESH,
        )
        c.start()
        started.append(c)

    def arrived(dst, half):
        pltpu.make_async_remote_copy(
            src_ref=buf.at[(dst,) + halves[half]],
            dst_ref=buf.at[(dst,) + halves[half]],
            send_sem=send.at[0],
            recv_sem=recv.at[dst, half],
            device_id=near["core"],
            device_id_type=MESH,
        ).wait_recv()

    for first in (0, 1):
        for a in axes:
            copy(0, item(a, 3, 0), first, (a, 1))
            copy(0, item(a, 1, 0), 1 - first, (a, -1))
    for half in (0, 1):
        copy(0, 1, half, "core")
    for a in axes:
        arrived(item(a, 3, 0), 0)
        copy(item(a, 3, 0), item(a, 2, 0), 0, (a, 1))
        arrived(item(a, 1, 0), 1)
        copy(item(a, 1, 0), item(a, 2, 0), 1, (a, -1))
    for a in axes:
        copy(item(a, 3, 0), item(a, 3, 1), 0, "core")
        copy(item(a, 1, 0), item(a, 1, 1), 1, "core")
    for a in axes:
        arrived(item(a, 3, 0), 1)
        copy(item(a, 3, 0), item(a, 3, 1), 1, "core")
        arrived(item(a, 1, 0), 0)
        copy(item(a, 1, 0), item(a, 1, 1), 0, "core")
    for a in axes:
        for half in (0, 1):
            arrived(item(a, 2, 0), half)
            copy(item(a, 2, 0), item(a, 2, 1), half, "core")
    for half in (0, 1):
        arrived(1, half)
        for a in axes:
            for d in (1, 2, 3):
                arrived(item(a, d, 1), half)
    for c in started:
        c.wait_send()


def encode(out, value):
    slots = value.shape[0]
    most = jnp.maximum(jnp.max(jnp.abs(value), axis=1), 1e-30)
    level = jnp.ceil(jnp.log2(most) * STEP)
    out[slots] = level.astype(jnp.int32).astype(jnp.int16)
    inverse = jnp.exp2(level * (-1.0 / STEP)) * TOP
    out[:slots] = jnp.round(value * inverse[:, None, :]).astype(jnp.int32).astype(jnp.int16)


def scales(code):
    return jnp.exp2(code.astype(jnp.int32).astype(jnp.float32) * (1.0 / STEP)) * (1.0 / TOP)


def decode(ref):
    slots = ref.shape[0] - 1
    scale = scales(ref[slots])
    return ref[:slots].astype(jnp.int32).astype(jnp.float32) * scale[:, None, :]


def kernel(
    nz, table, factors, out, blocks, partial, right_out, right_in, left_out, left_in, parts, scale,
    local, gsend, grecv, rsend, rrecv, lsend, lrecv, xsend, xrecv,
):
    y, x, q = place()
    z = lax.axis_index("narrow")
    rows = blocks.shape[2]
    chunk = rows // nz
    slots = partial.shape[0]
    up, down = lax.rem(z + 1, nz), lax.rem(z + nz - 1, nz)

    own = pltpu.make_async_copy(factors, blocks.at[0], local)
    own.start()
    barrier = pltpu.get_barrier_semaphore()
    for peer in (
        wide(y, lax.rem(x + 1, NX), q),
        wide(y, lax.rem(x + NX - 1, NX), q),
        wide(lax.rem(y + 1, NY), x, q),
        wide(lax.rem(y + NY - 1, NY), x, q),
        wide(y, x, 1 - q),
        {"narrow": up},
        {"narrow": down},
    ):
        pl.semaphore_signal(barrier, inc=1, device_id=peer, device_id_type=MESH)
    own.wait()
    pl.semaphore_wait(barrier, 7)

    cross_gather(blocks, ((0,), (1,)), ("x", "y"), gsend, grecv)

    def one(s, _):
        i, j = table[s], table[slots + s]
        contract = (((1,), (1,)), ((), ()))
        partial[s] = lax.dot_general(
            blocks[i, 0], blocks[j, 0], contract, preferred_element_type=jnp.float32
        ) + lax.dot_general(blocks[i, 1], blocks[j, 1], contract, preferred_element_type=jnp.float32)
        return 0

    lax.fori_loop(0, slots, one, 0)

    def mine(dest):
        return partial[:, pl.ds(pl.multiple_of(dest * chunk, chunk), chunk), :]

    def hop(src, dst, sends, recvs, t, to):
        return pltpu.make_async_remote_copy(
            src_ref=src.at[t],
            dst_ref=dst.at[t],
            send_sem=sends.at[t],
            recv_sem=recvs.at[t],
            device_id={"narrow": to},
            device_id_type=MESH,
        )

    nright, nleft = nz // 2, nz // 2 - 1
    rights = [hop(right_out, right_in, rsend, rrecv, t, up) for t in range(nright)]
    lefts = [hop(left_out, left_in, lsend, lrecv, t, down) for t in range(nleft)]
    for t in range(nright):
        value = mine(lax.rem(z + nz // 2 - t, nz))
        if t:
            rights[t - 1].wait_recv()
            value += decode(right_in.at[t - 1])
        encode(right_out.at[t], value)
        rights[t].start()
        if t < nleft:
            value = mine(lax.rem(z + nz - nleft + t, nz))
            if t:
                lefts[t - 1].wait_recv()
                value += decode(left_in.at[t - 1])
            encode(left_out.at[t], value)
            lefts[t].start()
    value = mine(z)
    lefts[-1].wait_recv()
    value += decode(left_in.at[nleft - 1])
    rights[-1].wait_recv()
    value += decode(right_in.at[nright - 1])
    encode(parts.at[0], value)

    cut = slots // 2
    cross_gather(parts, ((pl.ds(0, cut),), (pl.ds(cut, slots + 1 - cut),)), ("x",), xsend, xrecv)
    for k in range(parts.shape[0]):
        scale[k] = scales(parts[k, slots])
    nblk = out.shape[1] // rows
    for c in range(nblk):
        base = 2 * slots + 3 * c
        src, slot, live = table[base], table[base + 1], table[base + 2]
        tile = parts[src, slot].astype(jnp.int32).astype(jnp.float32) * scale[src, pl.ds(slot, 1), :]
        out[:, c * rows : (c + 1) * rows] = jnp.where(live > 0, tile, 0.0)
    for c in rights + lefts:
        c.wait_send()


def tables(pairs, turn):
    y, x, q = place()
    r, c = pairs[:, 0], pairs[:, 1]
    nblk = 2 * NX * NY
    node = (r // (2 * NX)) * NX + lax.rem(c // 2, NX)
    hot = (node[:, None] == jnp.arange(NX * NY)[None, :]).astype(jnp.int32)
    rank = jnp.sum((jnp.cumsum(hot, axis=0) - hot) * hot, axis=1)
    core, slot = lax.rem(rank, 2), rank // 2 - turn * SLOTS
    inside = (slot >= 0) & (slot < SLOTS)
    here = (node == y * NX + x) & (core == q) & inside
    pick = here[:, None] & (slot[:, None] == jnp.arange(SLOTS)[None, :])
    d = lax.rem(lax.rem(r // 2, NX) - x + NX, NX)
    row = 2 * d + (lax.rem(r, 2) ^ q)
    e = lax.rem(c // (2 * NX) - y + NY, NY)
    col = jnp.where(e == 0, 0, 2 * NX - 2 + 2 * e) + (lax.rem(c, 2) ^ q)
    row = jnp.sum(jnp.where(pick, row[:, None], 0), axis=0)
    col = jnp.sum(jnp.where(pick, col[:, None], 0), axis=0)
    want = (r == (y * NX + x) * 2 + q) & inside
    listed = want[:, None] & (c[:, None] == jnp.arange(nblk)[None, :])
    src = 2 * lax.rem(lax.rem(c // 2, NX) - x + NX, NX) + (core ^ q)
    found = [jnp.sum(jnp.where(listed, v[:, None], 0), axis=0) for v in (src, slot, jnp.ones_like(src))]
    return jnp.concatenate([row, col, jnp.stack(found, axis=1).reshape(-1)]), jnp.max(jnp.sum(hot, axis=0))


def shards(factors, pairs):
    nz = lax.axis_size("narrow")
    two, rows, occ = factors.shape
    nblk = lax.axis_size("wide")
    chunk = rows // nz
    nright, nleft = nz // 2, nz // 2 - 1
    code = (SLOTS + 1, chunk, rows)
    items = 2 * (NX + NY - 1)

    def run(table):
        return pl.pallas_call(
            functools.partial(kernel, nz),
            out_shape=jax.ShapeDtypeStruct((chunk, nblk * rows), jnp.float32),
            in_specs=[pl.BlockSpec(memory_space=pltpu.SMEM), pl.BlockSpec(memory_space=pl.ANY)],
            out_specs=pl.BlockSpec(memory_space=pltpu.VMEM),
            scratch_shapes=[
                pltpu.VMEM((items, two, rows, occ), jnp.bfloat16),
                pltpu.VMEM((SLOTS, rows, rows), jnp.float32),
                pltpu.VMEM((nright,) + code, jnp.int16),
                pltpu.VMEM((nright,) + code, jnp.int16),
                pltpu.VMEM((nleft,) + code, jnp.int16),
                pltpu.VMEM((nleft,) + code, jnp.int16),
                pltpu.VMEM((2 * NX,) + code, jnp.int16),
                pltpu.VMEM((2 * NX, SLOTS, rows), jnp.float32),
                pltpu.SemaphoreType.DMA,
                pltpu.SemaphoreType.DMA((26,)),
                pltpu.SemaphoreType.DMA((items, 2)),
                pltpu.SemaphoreType.DMA((nright,)),
                pltpu.SemaphoreType.DMA((nright,)),
                pltpu.SemaphoreType.DMA((nleft,)),
                pltpu.SemaphoreType.DMA((nleft,)),
                pltpu.SemaphoreType.DMA((14,)),
                pltpu.SemaphoreType.DMA((2 * NX, 2)),
            ],
            compiler_params=pltpu.CompilerParams(
                collective_id=0, has_side_effects=True, vmem_limit_bytes=48 * 1024 * 1024
            ),
        )(table, factors)

    table, most = tables(pairs, 0)
    out = run(table)
    return lax.cond(most > 2 * SLOTS, lambda o: o + run(tables(pairs, 1)[0]), lambda o: o, out)


def solution(mesh):
    placed = (P("narrow", "wide", None), P())
    return jax.shard_map(
        shards, mesh=mesh, in_specs=placed, out_specs=P(("wide", "narrow"), None), check_vma=False
    )
```

```python
import functools

import jax
import jax.numpy as jnp
from jax import lax
from jax.experimental import pallas as pl
from jax.experimental.pallas import tpu as pltpu
from jax.sharding import PartitionSpec as P

MESH = pl.DeviceIdType.MESH
NX = NY = 4
NODES = NX * NY
STREAMS = (3, 3, 3)
SLOTS = sum(STREAMS)
LANES = 128
STEP = 16.0
TOP = 32000.0
PATTERN = "skip"
BALANCE, FIXES = 4, 6


def place():
    w = lax.axis_index("wide")
    return w // (2 * NX), lax.rem(w // 2, NX), lax.rem(w, 2)


def wide(y, x, q):
    return {"wide": (y * NX + x) * 2 + q}


def item(axis, distance, other):
    if distance == 0:
        return other
    return (0 if axis == "x" else 2 * NX - 2) + 2 * distance + other


ITEMS = 2 * (NX + NY - 1)


def neighbours():
    y, x, q = place()
    return {
        ("x", 1): wide(y, lax.rem(x + 1, NX), q),
        ("x", -1): wide(y, lax.rem(x + NX - 1, NX), q),
        ("y", 1): wide(lax.rem(y + 1, NY), x, q),
        ("y", -1): wide(lax.rem(y + NY - 1, NY), x, q),
        "core": wide(y, x, 1 - q),
    }


def cross_gather(buf, halves, send, recv):
    near = neighbours()
    started = []

    def copy(src, dst, half, to):
        c = pltpu.make_async_remote_copy(
            src_ref=buf.at[(src,) + halves[half]],
            dst_ref=buf.at[(dst,) + halves[half]],
            send_sem=send.at[len(started)],
            recv_sem=recv.at[dst, half],
            device_id=near[to],
            device_id_type=MESH,
        )
        c.start()
        started.append(c)

    def arrived(dst, half):
        pltpu.make_async_remote_copy(
            src_ref=buf.at[(dst,) + halves[half]],
            dst_ref=buf.at[(dst,) + halves[half]],
            send_sem=send.at[0],
            recv_sem=recv.at[dst, half],
            device_id=near["core"],
            device_id_type=MESH,
        ).wait_recv()

    def start():
        for first in (0, 1):
            for a in "xy":
                copy(0, item(a, 3, 0), first, (a, 1))
                copy(0, item(a, 1, 0), 1 - first, (a, -1))
        for half in (0, 1):
            copy(0, 1, half, "core")

    def relay():
        for a in "xy":
            arrived(item(a, 3, 0), 0)
            copy(item(a, 3, 0), item(a, 2, 0), 0, (a, 1))
            arrived(item(a, 1, 0), 1)
            copy(item(a, 1, 0), item(a, 2, 0), 1, (a, -1))
        for a in "xy":
            copy(item(a, 3, 0), item(a, 3, 1), 0, "core")
            copy(item(a, 1, 0), item(a, 1, 1), 1, "core")
        for a in "xy":
            arrived(item(a, 3, 0), 1)
            copy(item(a, 3, 0), item(a, 3, 1), 1, "core")
            arrived(item(a, 1, 0), 0)
            copy(item(a, 1, 0), item(a, 1, 1), 0, "core")
        for half in (0, 1):
            for a in "xy":
                arrived(item(a, 2, 0), half)
                copy(item(a, 2, 0), item(a, 2, 1), half, "core")

    def finish():
        for half in (0, 1):
            arrived(1, half)
            for a in "xy":
                for d in (1, 3, 2):
                    arrived(item(a, d, 1), half)
        for c in started:
            c.wait_send()

    return start, relay, finish


def encode(out, value):
    g = value.shape[0]
    rows = out.shape[1]
    halves = [value[:, :, :LANES], value[:, :, LANES:]]
    most = jnp.concatenate(
        [jnp.max(jnp.abs(h), axis=1) for h in halves] + [jnp.zeros((rows - 2 * g, LANES), jnp.float32)], axis=0
    )
    level = jnp.ceil(jnp.log2(jnp.maximum(most, 1e-30)) * STEP)
    out[2 * g] = level.astype(jnp.int32).astype(jnp.int16)
    inverse = jnp.exp2(level * (-1.0 / STEP)) * TOP
    for k in range(2):
        scaled = jnp.round(halves[k] * inverse[k * g : (k + 1) * g][:, None, :])
        out[k * g : (k + 1) * g] = scaled.astype(jnp.int32).astype(jnp.int16)


def scales(code):
    return jnp.exp2(code.astype(jnp.int32).astype(jnp.float32) * (1.0 / STEP)) * (1.0 / TOP)


def decode(ref):
    g = ref.shape[0] // 2
    scale = scales(ref[2 * g])
    tiles = ref[: 2 * g].astype(jnp.int32).astype(jnp.float32) * scale[: 2 * g][:, None, :]
    return jnp.concatenate([tiles[:g], tiles[g:]], axis=2)


def summed(value, axis):
    return jnp.sum(value, axis=axis, keepdims=True)


def balance(lo, hi):
    up = lax.broadcasted_iota(jnp.int32, (NODES, NODES), 0)
    across = lax.broadcasted_iota(jnp.int32, (NODES, NODES), 1)
    chip = lax.broadcasted_iota(jnp.int32, (NODES, lo.shape[1]), 0)
    is_lo = (chip == lo).astype(jnp.float32)
    is_hi = (chip == hi).astype(jnp.float32)
    lanes = (((1,), (1,)), ((), ()))
    count = lax.dot_general(is_lo, is_hi, lanes, preferred_element_type=jnp.float32)
    count += lax.dot_general(is_hi, is_lo, lanes, preferred_element_type=jnp.float32)
    same = up == across
    loops = jnp.where(same, count * 0.5, 0.0)
    count = jnp.where(same, 0.0, count)
    loops_up, loops_across = summed(loops, 1), summed(loops, 0)

    def loads(give):
        return summed(give, 1) + loops_up, summed(count - give, 0) + loops_across

    give = count * 0.5
    for _ in range(BALANCE):
        load_up, load_across = loads(give)
        give = jnp.clip(give - (load_up - load_across) * (1.0 / NODES), 0.0, count)
    give = jnp.where(up < across, jnp.floor(give + 0.5), count - jnp.floor(count - give + 0.5))
    tag_up, tag_across = up.astype(jnp.float32), across.astype(jnp.float32)
    for _ in range(FIXES):
        load_up, load_across = loads(give)
        full_up, full_across = load_up * 64.0 + tag_up, load_across * 64.0 + tag_across
        full = jnp.max(jnp.max(full_across, axis=1, keepdims=True), axis=0, keepdims=True)
        target = jnp.where((full_up == full) & (give > 0.0), full_across, 1e9)
        mirror = jnp.where((full_across == full) & (count - give > 0.0), full_up, 1e9)
        least = jnp.min(jnp.min(target, axis=1, keepdims=True), axis=0, keepdims=True)
        move = (full - least >= 128.0).astype(jnp.float32)
        give = give - jnp.where(target == least, move, 0.0) + jnp.where(mirror == least, move, 0.0)
    load_up, load_across = loads(give)
    most = jnp.max(load_across, axis=1, keepdims=True)
    return give, is_lo, is_hi, most


def earlier(key):
    n = key.shape[1]
    up = lax.broadcasted_iota(jnp.int32, (n, n), 0)
    across = lax.broadcasted_iota(jnp.int32, (n, n), 1)
    column = summed(jnp.where(up == across, key, 0), 1)
    return summed(jnp.where((column == key) & (up < across), 1, 0), 0), column, up == across


def tables(pairs, turn):
    y, x, q = place()
    r, c = pairs[0:1, :], pairs[1:2, :]
    yr, xr, yc, xc = r >> 3, (r >> 1) & 3, c >> 3, (c >> 1) & 3
    one, two = yr * NX + xc, yc * NX + xr
    lo, hi = jnp.minimum(one, two), jnp.maximum(one, two)
    give, is_lo, is_hi, most = balance(lo, hi)
    share = lax.dot_general(give, is_lo, (((0,), (0,)), ((), ())), preferred_element_type=jnp.float32)
    share = summed(share * is_hi, 0)
    rank = earlier(lo * NODES + hi)[0]
    node = jnp.where(rank.astype(jnp.float32) < share, lo, hi)
    rank, node, same = earlier(node)

    def column(v):
        return summed(jnp.where(same, v, 0), 1)

    r, c, rank = column(r), column(c), column(rank)
    core, slot = rank & 1, (rank >> 1) - turn * SLOTS
    lane = lax.broadcasted_iota(jnp.int32, (r.shape[0], LANES), 1)

    def seen(block_y, block_x, other):
        along = 2 * ((block_x - x) & (NX - 1)) + other
        across = jnp.where(block_y == y, 0, 2 * NX - 2) + 2 * ((block_y - y) & (NY - 1)) + other
        return jnp.where(block_y == y, along, across)

    pick = (node == y * NX + x) & (core == q) & (slot == lane)
    rows = summed(jnp.where(pick, seen(r >> 3, (r >> 1) & 3, (r & 1) ^ q), 0), 0)
    cols = summed(jnp.where(pick, seen(c >> 3, (c >> 1) & 3, (c & 1) ^ q), 0), 0)
    want = (r == (y * NX + x) * 2 + q) & (slot >= 0) & (slot < SLOTS) & (c == lane)
    src = summed(jnp.where(want, seen(node >> 2, node & 3, core ^ q), 0), 0)
    at = summed(jnp.where(want, slot, 0), 0)
    live = summed(jnp.where(want, 1, 0), 0)
    rows, cols, src = [jnp.minimum(v, ITEMS - 1) for v in (rows, cols, src)]
    return (rows, cols, src, jnp.minimum(at, SLOTS - 1), live), most


def trees(nz):
    far = (nz // 2, nz // 2 - 1)
    if PATTERN == "ring":
        return [{k: k - 1 for k in range(1, n + 1)} for n in far]
    return [{k: max(k - 2 + k % 2, 0) for k in range(1, n + 1)} for n in far]


def kernel(
    nz, turn, pairs, factors, out, most_out, blocks, partial, z_out, z_in, parts, scale, table, table_s,
    local, gsend, grecv, zsend, zrecv, xsend, xrecv,
):
    z = lax.axis_index("narrow")
    rows = blocks.shape[2]
    chunk = rows // nz
    tree = trees(nz)
    starts = [sum(STREAMS[:s]) for s in range(len(STREAMS))]

    def away(d):
        return {"narrow": lax.rem(z + d + nz, nz)}

    own = pltpu.make_async_copy(factors, blocks.at[0], local)
    own.start()
    barrier = pltpu.get_barrier_semaphore()
    hops = sorted({sign * (k - p) for t in tree for k, p in t.items() for sign in (1, -1)})
    peers = list(neighbours().values()) + [away(d) for d in hops]
    for peer in peers:
        pl.semaphore_signal(barrier, inc=1, device_id=peer, device_id_type=MESH)
    own.wait()
    pl.semaphore_wait(barrier, len(peers))

    start, relay, finish = cross_gather(blocks, ((0,), (1,)), gsend, grecv)
    start()
    lists, most = tables(pairs[...], turn[0])
    for k, v in enumerate(lists):
        table[k : k + 1, :] = v
    most_out[...] = jnp.broadcast_to(most, most_out.shape)
    scalars = pltpu.make_async_copy(table, table_s, local)
    scalars.start()
    relay()
    scalars.wait()
    finish()

    def make(s, _):
        i, j = table_s[0, s], table_s[1, s]
        contract = (((1,), (1,)), ((), ()))
        partial[s] = lax.dot_general(
            blocks[i, 0], blocks[j, 0], contract, preferred_element_type=jnp.float32
        ) + lax.dot_general(blocks[i, 1], blocks[j, 1], contract, preferred_element_type=jnp.float32)
        return 0

    def span(stream):
        at = 2 * starts[stream] + stream
        return pl.ds(at, 2 * STREAMS[stream] + 1)

    def mine(dest, stream):
        at = pl.multiple_of(dest * chunk, chunk)
        return partial[pl.ds(starts[stream], STREAMS[stream]), pl.ds(at, chunk), :]

    def hop(side, k, stream):
        buf = side * (nz // 2) + k - 1
        return pltpu.make_async_remote_copy(
            src_ref=z_out.at[buf, span(stream)],
            dst_ref=z_in.at[buf, span(stream)],
            send_sem=zsend.at[buf, stream],
            recv_sem=zrecv.at[buf, stream],
            device_id=away((1, -1)[side] * (k - tree[side][k])),
            device_id_type=MESH,
        )

    sent = []

    def gathered(side, k, stream, value):
        for child, parent in sorted(tree[side].items(), reverse=True):
            if parent == k:
                hop(side, child, stream).wait_recv()
                value += decode(z_in.at[side * (nz // 2) + child - 1, span(stream)])
        return value

    def send(side, k, stream):
        dest = lax.rem(z + (1, -1)[side] * k + nz, nz)
        value = gathered(side, k, stream, mine(dest, stream))
        encode(z_out.at[side * (nz // 2) + k - 1, span(stream)], value)
        c = hop(side, k, stream)
        c.start()
        sent.append(c)

    for k in range(nz // 2, 0, -1):
        for stream in range(len(STREAMS)):
            if k == nz // 2:
                lax.fori_loop(starts[stream], starts[stream] + STREAMS[stream], make, 0)
            for side in (0, 1):
                if k in tree[side]:
                    send(side, k, stream)
    for stream in range(len(STREAMS)):
        value = mine(z, stream)
        for side in (1, 0):
            value = gathered(side, 0, stream, value)
        encode(parts.at[0, span(stream)], value)

    tiles = parts.shape[1]
    cut = tiles // 2
    start, relay, finish = cross_gather(parts, ((pl.ds(0, cut),), (pl.ds(cut, tiles - cut),)), xsend, xrecv)
    start()
    relay()
    finish()
    for k in range(ITEMS):
        for stream, g in enumerate(STREAMS):
            s = scales(parts[k, 2 * starts[stream] + stream + 2 * g])
            for j in range(g):
                scale[k * SLOTS + starts[stream] + j, 0:1, :] = s[j : j + 1]
                scale[k * SLOTS + starts[stream] + j, 1:2, :] = s[g + j : g + j + 1]
    nblk = out.shape[1] // rows
    for c in range(nblk):
        src, slot, live = table_s[2, c], table_s[3, c], table_s[4, c]
        first, step = slot, STREAMS[0]
        for stream in range(1, len(STREAMS)):
            later = slot >= starts[stream]
            first = jnp.where(later, slot + starts[stream] + stream, first)
            step = jnp.where(later, STREAMS[stream], step)
        s = scale[src * SLOTS + slot]
        for h in range(2):
            tile = parts[src, first + h * step].astype(jnp.int32).astype(jnp.float32) * s[h : h + 1]
            out[:, c * rows + h * LANES : c * rows + (h + 1) * LANES] = jnp.where(live > 0, tile, 0.0)
    for c in sent:
        c.wait_send()


def shards(factors, pairs):
    nz = lax.axis_size("narrow")
    two, rows, occ = factors.shape
    nblk = lax.axis_size("wide")
    chunk = rows // nz
    tiles = 2 * SLOTS + len(STREAMS)
    hops = (nz - 1, len(STREAMS))
    pairs = pairs.T

    def run(turn):
        return pl.pallas_call(
            functools.partial(kernel, nz),
            out_shape=(
                jax.ShapeDtypeStruct((chunk, nblk * rows), jnp.float32),
                jax.ShapeDtypeStruct((8, LANES), jnp.float32),
            ),
            in_specs=[
                pl.BlockSpec(memory_space=pltpu.SMEM),
                pl.BlockSpec(memory_space=pltpu.VMEM),
                pl.BlockSpec(memory_space=pl.ANY),
            ],
            out_specs=[pl.BlockSpec(memory_space=pltpu.VMEM)] * 2,
            scratch_shapes=[
                pltpu.VMEM((ITEMS, two, rows, occ), jnp.bfloat16),
                pltpu.VMEM((SLOTS, rows, rows), jnp.float32),
                pltpu.VMEM((nz - 1, tiles, chunk, LANES), jnp.int16),
                pltpu.VMEM((nz - 1, tiles, chunk, LANES), jnp.int16),
                pltpu.VMEM((ITEMS, tiles, chunk, LANES), jnp.int16),
                pltpu.VMEM((ITEMS * SLOTS, 8, LANES), jnp.float32),
                pltpu.VMEM((8, LANES), jnp.int32),
                pltpu.SMEM((8, LANES), jnp.int32),
                pltpu.SemaphoreType.DMA,
                pltpu.SemaphoreType.DMA((2 * ITEMS - 2,)),
                pltpu.SemaphoreType.DMA((ITEMS, 2)),
                pltpu.SemaphoreType.DMA(hops),
                pltpu.SemaphoreType.DMA(hops),
                pltpu.SemaphoreType.DMA((2 * ITEMS - 2,)),
                pltpu.SemaphoreType.DMA((ITEMS, 2)),
            ],
            compiler_params=pltpu.CompilerParams(
                collective_id=0, has_side_effects=True, vmem_limit_bytes=48 * 1024 * 1024
            ),
        )(turn, pairs, factors)

    out, most = run(jnp.zeros((1,), jnp.int32))
    most = most[0, 0]

    def more(state):
        return state[0].astype(jnp.float32) * (2 * SLOTS) < most

    def again(state):
        turn, out = state
        return turn + 1, out + run(turn[None])[0]

    return lax.while_loop(more, again, (jnp.int32(1), out))[1]


def solution(mesh):
    placed = (P("narrow", "wide", None), P())
    return jax.shard_map(
        shards, mesh=mesh, in_specs=placed, out_specs=P(("wide", "narrow"), None), check_vma=False
    )
```

```python
import functools

import jax
import jax.numpy as jnp
from jax import lax
from jax.experimental import pallas as pl
from jax.experimental.pallas import tpu as pltpu
from jax.sharding import PartitionSpec as P

MESH = pl.DeviceIdType.MESH
NX = NY = 4
NODES = NX * NY
EARLY, LATE = (5,), (4,)
STREAMS = EARLY + LATE
HEAD, TAIL = sum(EARLY), sum(LATE)
SLOTS = HEAD + TAIL
LANES = 128
STEP = 16.0
TOP = 32000.0
ROUTES = ("skip", 0), ("skip", 1)
STEPS = (0, (6, 3)), (1, (6, 3)), (0, (4, 1)), (1, (4, 1)), (0, (2,)), (1, (2,))
FIRST = (8, 7, 5), (8, 7, 5)
BALANCE, FIXES = 4, 6


def place():
    w = lax.axis_index("wide")
    return w // (2 * NX), lax.rem(w // 2, NX), lax.rem(w, 2)


def wide(y, x, q):
    return {"wide": (y * NX + x) * 2 + q}


NEAR = 10


def item(axis, distance, other):
    if distance == 0:
        return other
    if distance == 2:
        return NEAR + "xy".index(axis) * 2 + other
    return 2 + "xy".index(axis) * 4 + (distance - 1) + other


ITEMS = 2 * (NX + NY - 1)


def neighbours():
    y, x, q = place()
    return {
        ("x", 1): wide(y, lax.rem(x + 1, NX), q),
        ("x", -1): wide(y, lax.rem(x + NX - 1, NX), q),
        ("y", 1): wide(lax.rem(y + 1, NY), x, q),
        ("y", -1): wide(lax.rem(y + NY - 1, NY), x, q),
        ("x", 2): wide(y, lax.rem(x + 2, NX), q),
        ("y", 2): wide(lax.rem(y + 2, NY), x, q),
        "core": wide(y, x, 1 - q),
    }


def courier(view, pieces, send, recv):
    near = neighbours()
    started = []

    def both(src, dst, piece, to, sem):
        cut, at = pieces[piece]
        return pltpu.make_async_remote_copy(
            src_ref=view(src, cut),
            dst_ref=view(dst, cut),
            send_sem=send.at[sem],
            recv_sem=recv.at[dst, at],
            device_id=near[to],
            device_id_type=MESH,
        )

    def copy(src, dst, piece, to):
        c = both(src, dst, piece, to, len(started))
        c.start()
        started.append(c)

    def arrived(dst, piece):
        both(dst, dst, piece, "core", 0).wait_recv()

    def drain():
        for c in started:
            c.wait_send()

    return copy, arrived, drain


def gather_blocks(close, distant, send, recv):
    def view(k, cut):
        return close.at[(k,) + cut] if k < NEAR else distant.at[(k - NEAR,) + cut]

    copy, arrived, drain = courier(view, (((0,), 0), ((1,), 1)), send, recv)

    def start():
        for first in (0, 1):
            for a in "xy":
                copy(0, item(a, 3, 0), first, (a, 1))
                copy(0, item(a, 1, 0), 1 - first, (a, -1))
        for half in (0, 1):
            copy(0, 1, half, "core")

    def relay():
        for a in "xy":
            arrived(item(a, 3, 0), 0)
            copy(item(a, 3, 0), item(a, 2, 0), 0, (a, 1))
            arrived(item(a, 1, 0), 1)
            copy(item(a, 1, 0), item(a, 2, 0), 1, (a, -1))
        for a in "xy":
            copy(item(a, 3, 0), item(a, 3, 1), 0, "core")
            copy(item(a, 1, 0), item(a, 1, 1), 1, "core")

    def near():
        for a in "xy":
            arrived(item(a, 3, 0), 1)
            copy(item(a, 3, 0), item(a, 3, 1), 1, "core")
            arrived(item(a, 1, 0), 0)
            copy(item(a, 1, 0), item(a, 1, 1), 0, "core")
        for half in (0, 1):
            arrived(1, half)
            for a in "xy":
                arrived(item(a, 1, 1), half)
                arrived(item(a, 3, 1), half)

    def far():
        for half in (0, 1):
            for a in "xy":
                arrived(item(a, 2, 0), half)
                copy(item(a, 2, 0), item(a, 2, 1), half, "core")

    def finish():
        for half in (0, 1):
            for a in "xy":
                arrived(item(a, 2, 1), half)
        drain()

    return start, relay, near, far, finish


def exchange(buf, first, size, send, recv):
    cut = size // 2
    pieces = ((pl.ds(first, size),), 0), ((pl.ds(first, cut),), 0), ((pl.ds(first + cut, size - cut),), 1)
    copy, arrived, drain = courier(lambda k, cut: buf.at[(k,) + cut], pieces, send, recv)

    def start():
        for a in "xy":
            copy(0, item(a, 2, 0), 0, (a, 2))
        for a in "xy":
            copy(0, item(a, 3, 0), 0, (a, 1))
            copy(0, item(a, 1, 0), 0, (a, -1))
        copy(0, 1, 0, "core")

    def relay():
        for a in "xy":
            arrived(item(a, 3, 0), 0)
            copy(item(a, 3, 0), item(a, 3, 1), 0, "core")
            arrived(item(a, 1, 0), 0)
            copy(item(a, 1, 0), item(a, 1, 1), 0, "core")

    def far():
        for a in "xy":
            arrived(item(a, 2, 0), 0)
            copy(item(a, 2, 0), item(a, 2, 1), 0, "core")

    def finish():
        arrived(1, 0)
        for a in "xy":
            for d in (1, 3, 2):
                arrived(item(a, d, 1), 0)
        drain()

    return start, relay, far, finish


def encode(out, value):
    g = value.shape[0]
    rows = out.shape[1]
    halves = [value[:, :, :LANES], value[:, :, LANES:]]
    most = jnp.concatenate(
        [jnp.max(jnp.abs(h), axis=1) for h in halves] + [jnp.zeros((rows - 2 * g, LANES), jnp.float32)], axis=0
    )
    level = jnp.ceil(jnp.log2(jnp.maximum(most, 1e-30)) * STEP)
    out[2 * g] = level.astype(jnp.int32).astype(jnp.int16)
    inverse = jnp.exp2(level * (-1.0 / STEP)) * TOP
    for k in range(2):
        scaled = jnp.round(halves[k] * inverse[k * g : (k + 1) * g][:, None, :])
        out[k * g : (k + 1) * g] = scaled.astype(jnp.int32).astype(jnp.int16)


def scales(code):
    return jnp.exp2(code.astype(jnp.int32).astype(jnp.float32) * (1.0 / STEP)) * (1.0 / TOP)


def decode(ref):
    g = ref.shape[0] // 2
    scale = scales(ref[2 * g])
    tiles = ref[: 2 * g].astype(jnp.int32).astype(jnp.float32) * scale[: 2 * g][:, None, :]
    return jnp.concatenate([tiles[:g], tiles[g:]], axis=2)


def summed(value, axis):
    return jnp.sum(value, axis=axis, keepdims=True)


def balance(lo, hi, chosen):
    up = lax.broadcasted_iota(jnp.int32, (NODES, NODES), 0)
    across = lax.broadcasted_iota(jnp.int32, (NODES, NODES), 1)
    chip = lax.broadcasted_iota(jnp.int32, (NODES, lo.shape[1]), 0)
    is_lo = ((chip == lo) & chosen).astype(jnp.float32)
    is_hi = ((chip == hi) & chosen).astype(jnp.float32)
    lanes = (((1,), (1,)), ((), ()))
    count = lax.dot_general(is_lo, is_hi, lanes, preferred_element_type=jnp.float32)
    count += lax.dot_general(is_hi, is_lo, lanes, preferred_element_type=jnp.float32)
    same = up == across
    loops = jnp.where(same, count * 0.5, 0.0)
    count = jnp.where(same, 0.0, count)
    loops_up, loops_across = summed(loops, 1), summed(loops, 0)

    def loads(give):
        return summed(give, 1) + loops_up, summed(count - give, 0) + loops_across

    give = count * 0.5
    for _ in range(BALANCE):
        load_up, load_across = loads(give)
        give = jnp.clip(give - (load_up - load_across) * (1.0 / NODES), 0.0, count)
    give = jnp.where(up < across, jnp.floor(give + 0.5), count - jnp.floor(count - give + 0.5))
    tag_up, tag_across = up.astype(jnp.float32), across.astype(jnp.float32)
    for _ in range(FIXES):
        load_up, load_across = loads(give)
        full_up, full_across = load_up * 64.0 + tag_up, load_across * 64.0 + tag_across
        full = jnp.max(jnp.max(full_across, axis=1, keepdims=True), axis=0, keepdims=True)
        target = jnp.where((full_up == full) & (give > 0.0), full_across, 1e9)
        mirror = jnp.where((full_across == full) & (count - give > 0.0), full_up, 1e9)
        least = jnp.min(jnp.min(target, axis=1, keepdims=True), axis=0, keepdims=True)
        move = (full - least >= 128.0).astype(jnp.float32)
        give = give - jnp.where(target == least, move, 0.0) + jnp.where(mirror == least, move, 0.0)
    share = lax.dot_general(give, is_lo, (((0,), (0,)), ((), ())), preferred_element_type=jnp.float32)
    return summed(share * is_hi, 0)


def tables(pairs, turn):
    y, x, q = place()
    n = pairs.shape[1]
    up = lax.broadcasted_iota(jnp.int32, (n, n), 0)
    across = lax.broadcasted_iota(jnp.int32, (n, n), 1)
    same, before = up == across, up < across

    def column(v):
        return summed(jnp.where(same, v, 0), 1)

    def ranks(key):
        return summed(jnp.where((column(key) == key) & before, 1, 0), 0)

    r, c = pairs[0:1, :], pairs[1:2, :]
    yr, xr, yc, xc = r >> 3, (r >> 1) & 3, c >> 3, (c >> 1) & 3
    far_x, far_y = ((xr - xc) & 3) == 2, ((yr - yc) & 3) == 2
    middle_x, middle_y = far_x & (yr == yc), far_y & (xr == xc)
    late = (far_x | far_y) & jnp.logical_not(middle_x | middle_y)
    kind = late.astype(jnp.int32)
    one, two = yr * NX + xc, yc * NX + xr
    one = jnp.where(middle_x, yr * NX + ((xr + 1) & 3), jnp.where(middle_y, ((yr + 1) & 3) * NX + xr, one))
    two = jnp.where(middle_x, yr * NX + ((xr + 3) & 3), jnp.where(middle_y, ((yr + 3) & 3) * NX + xr, two))
    lo, hi = jnp.minimum(one, two), jnp.maximum(one, two)
    share = jnp.where(late, balance(lo, hi, late), balance(lo, hi, jnp.logical_not(late)))
    rank = ranks((lo * NODES + hi) * 2 + kind)
    node = jnp.where(rank.astype(jnp.float32) < share, lo, hi)
    rank = ranks(node * 2 + kind)
    node_up = column(node)
    ahead = summed(jnp.where((node_up == node) & (column(kind) == 0), 1, 0), 0)
    rank = jnp.where(late, jnp.maximum(ahead, 2 * HEAD) + rank, rank)
    most = jnp.broadcast_to(jnp.max(rank, axis=1, keepdims=True) + 1, (1, LANES))

    r, c, node, rank = column(r), column(c), node_up, column(rank)
    core, slot = rank & 1, (rank >> 1) - turn * TAIL
    inside = (slot >= jnp.where(turn > 0, HEAD, 0)) & (slot < SLOTS)
    lane = lax.broadcasted_iota(jnp.int32, (r.shape[0], LANES), 1)

    def seen(block_y, block_x, other):
        aside = block_y != y
        d = jnp.where(aside, block_y - y, block_x - x) & 3
        line = aside.astype(jnp.int32)
        return other + jnp.where(d == 0, 0, jnp.where(d == 2, NEAR + 2 * line, 1 + 4 * line + d))

    pick = (node == y * NX + x) & (core == q) & inside & (slot == lane)
    rows = summed(jnp.where(pick, seen(r >> 3, (r >> 1) & 3, (r & 1) ^ q), 0), 0)
    cols = summed(jnp.where(pick, seen(c >> 3, (c >> 1) & 3, (c & 1) ^ q), 0), 0)
    want = (r == (y * NX + x) * 2 + q) & inside & (c == lane)
    src = summed(jnp.where(want, seen(node >> 2, node & 3, core ^ q), 0), 0)
    at = summed(jnp.where(want, slot, 0), 0)
    live = summed(jnp.where(want, 1, 0), 0)
    rows, cols, src = [jnp.minimum(v, ITEMS - 1) for v in (rows, cols, src)]
    return rows, cols, src, jnp.minimum(at, SLOTS - 1), live, most


PARENTS = {
    "ring": {k: k - 1 for k in range(1, 9)},
    "skip": {8: 6, 7: 6, 6: 4, 5: 4, 4: 2, 3: 2, 2: 0, 1: 0},
    "mix": {8: 6, 7: 6, 6: 4, 5: 4, 4: 2, 3: 2, 2: 1, 1: 0},
}


def trees(group):
    pattern, longer = ROUTES[group]
    return [{k: p for k, p in PARENTS[pattern].items() if k < 8 or side == longer} for side in (0, 1)]


def kernel(
    nz, turn, pairs, factors, out, most_out, close, distant, partial, z_out, z_in, parts, scale, table, table_s,
    local, gsend, grecv, zsend, zrecv, xsend, xrecv,
):
    z = lax.axis_index("narrow")
    rows = close.shape[2]
    chunk = rows // nz
    forest = [trees(0)] * len(EARLY) + [trees(1)] * len(LATE)
    starts = [sum(STREAMS[:s]) for s in range(len(STREAMS))]

    def away(d):
        return {"narrow": lax.rem(z + d + nz, nz)}

    own = pltpu.make_async_copy(factors, close.at[0], local)
    own.start()
    barrier = pltpu.get_barrier_semaphore()
    hops = sorted({sign * (k - p) for trees in forest for t in trees for k, p in t.items() for sign in (1, -1)})
    peers = list(neighbours().values()) + [away(d) for d in hops]
    for peer in peers:
        pl.semaphore_signal(barrier, inc=1, device_id=peer, device_id_type=MESH)
    own.wait()
    pl.semaphore_wait(barrier, len(peers))

    start, relay, near, far, finish = gather_blocks(close, distant, gsend, grecv)
    start()
    for k, v in enumerate(tables(pairs[...], turn[0])):
        table[k : k + 1, :] = v
    scalars = pltpu.make_async_copy(table, table_s, local)
    scalars.start()
    relay()
    scalars.wait()
    most_out[0] = table_s[5, 0]

    def tile(s, load):
        i, j = table_s[0, s], table_s[1, s]
        contract = (((1,), (1,)), ((), ()))
        partial[s] = sum(
            lax.dot_general(load(i, p), load(j, p), contract, preferred_element_type=jnp.float32) for p in (0, 1)
        )

    def load_close(i, p):
        return close[jnp.minimum(i, NEAR - 1), p]

    def load_any(i, p):
        return jnp.where(i < NEAR, load_close(i, p), distant[jnp.maximum(i - NEAR, 0), p])

    def span(stream):
        at = 2 * starts[stream] + stream
        return pl.ds(at, 2 * STREAMS[stream] + 1)

    def mine(dest, stream):
        at = pl.multiple_of(dest * chunk, chunk)
        return partial[pl.ds(starts[stream], STREAMS[stream]), pl.ds(at, chunk), :]

    def hop(side, k, stream):
        buf = side * (nz // 2) + k - 1
        return pltpu.make_async_remote_copy(
            src_ref=z_out.at[buf, span(stream)],
            dst_ref=z_in.at[buf, span(stream)],
            send_sem=zsend.at[buf, stream],
            recv_sem=zrecv.at[buf, stream],
            device_id=away((1, -1)[side] * (k - forest[stream][side][k])),
            device_id_type=MESH,
        )

    sent = []

    def gathered(side, k, stream, value):
        for child, parent in sorted(forest[stream][side].items(), reverse=True):
            if parent == k:
                hop(side, child, stream).wait_recv()
                value += decode(z_in.at[side * (nz // 2) + child - 1, span(stream)])
        return value

    def send(side, k, stream):
        dest = lax.rem(z + (1, -1)[side] * k + nz, nz)
        value = gathered(side, k, stream, mine(dest, stream))
        encode(z_out.at[side * (nz // 2) + k - 1, span(stream)], value)
        c = hop(side, k, stream)
        c.start()
        sent.append(c)

    def leg(ks, streams):
        for stream in streams:
            for k in ks:
                for side in (0, 1):
                    if k in forest[stream][side]:
                        send(side, k, stream)

    def make(streams, load):
        def one(s, _):
            tile(s, load)
            return 0

        for stream in streams:
            lax.fori_loop(starts[stream], starts[stream] + STREAMS[stream], one, 0)

    groups = (range(len(EARLY)), range(len(EARLY), len(STREAMS)))
    near()
    make(groups[0], load_close)
    leg(FIRST[0], groups[0])
    far()
    finish()
    make(groups[1], load_any)
    leg(FIRST[1], groups[1])
    for group, ks in STEPS:
        leg(ks, groups[group])
    swaps = []
    for stream, g in enumerate(STREAMS):
        value = mine(z, stream)
        for side in (1, 0):
            value = gathered(side, 0, stream, value)
        encode(parts.at[0, span(stream)], value)
        swaps.append(exchange(parts, 2 * starts[stream] + stream, 2 * g + 1, xsend.at[stream], xrecv.at[stream]))
        swaps[-1][0]()
    for swap in swaps:
        swap[1]()
    for swap in swaps:
        swap[2]()
    for swap in swaps:
        swap[3]()
    for k in range(ITEMS):
        for stream, g in enumerate(STREAMS):
            s = scales(parts[k, 2 * starts[stream] + stream + 2 * g])
            for j in range(g):
                scale[k * SLOTS + starts[stream] + j, 0:1, :] = s[j : j + 1]
                scale[k * SLOTS + starts[stream] + j, 1:2, :] = s[g + j : g + j + 1]
    nblk = out.shape[1] // rows
    for c in range(nblk):
        src, slot, live = table_s[2, c], table_s[3, c], table_s[4, c]
        first, step = slot, STREAMS[0]
        for stream in range(1, len(STREAMS)):
            later = slot >= starts[stream]
            first = jnp.where(later, slot + starts[stream] + stream, first)
            step = jnp.where(later, STREAMS[stream], step)
        s = scale[src * SLOTS + slot]
        for h in range(2):
            found = parts[src, first + h * step].astype(jnp.int32).astype(jnp.float32) * s[h : h + 1]
            out[:, c * rows + h * LANES : c * rows + (h + 1) * LANES] = jnp.where(live > 0, found, 0.0)
    for c in sent:
        c.wait_send()


def shards(factors, pairs):
    nz = lax.axis_size("narrow")
    two, rows, occ = factors.shape
    nblk = lax.axis_size("wide")
    chunk = rows // nz
    tiles = 2 * SLOTS + len(STREAMS)
    hops = (nz, len(STREAMS))
    pairs = pairs.T

    def run(turn):
        return pl.pallas_call(
            functools.partial(kernel, nz),
            out_shape=(
                jax.ShapeDtypeStruct((chunk, nblk * rows), jnp.float32),
                jax.ShapeDtypeStruct((1,), jnp.int32),
            ),
            in_specs=[
                pl.BlockSpec(memory_space=pltpu.SMEM),
                pl.BlockSpec(memory_space=pltpu.VMEM),
                pl.BlockSpec(memory_space=pl.ANY),
            ],
            out_specs=[pl.BlockSpec(memory_space=pltpu.VMEM), pl.BlockSpec(memory_space=pltpu.SMEM)],
            scratch_shapes=[
                pltpu.VMEM((NEAR, two, rows, occ), jnp.bfloat16),
                pltpu.VMEM((ITEMS - NEAR, two, rows, occ), jnp.bfloat16),
                pltpu.VMEM((SLOTS, rows, rows), jnp.float32),
                pltpu.VMEM((nz, tiles, chunk, LANES), jnp.int16),
                pltpu.VMEM((nz, tiles, chunk, LANES), jnp.int16),
                pltpu.VMEM((ITEMS, tiles, chunk, LANES), jnp.int16),
                pltpu.VMEM((ITEMS * SLOTS, 8, LANES), jnp.float32),
                pltpu.VMEM((8, LANES), jnp.int32),
                pltpu.SMEM((8, LANES), jnp.int32),
                pltpu.SemaphoreType.DMA,
                pltpu.SemaphoreType.DMA((2 * ITEMS - 2,)),
                pltpu.SemaphoreType.DMA((ITEMS, 2)),
                pltpu.SemaphoreType.DMA(hops),
                pltpu.SemaphoreType.DMA(hops),
                pltpu.SemaphoreType.DMA((len(STREAMS), 15)),
                pltpu.SemaphoreType.DMA((len(STREAMS), ITEMS, 2)),
            ],
            compiler_params=pltpu.CompilerParams(
                collective_id=0, has_side_effects=True, vmem_limit_bytes=48 * 1024 * 1024
            ),
        )(turn, pairs, factors)

    out, most = run(jnp.zeros((1,), jnp.int32))

    def more(state):
        return most[0] > 2 * (HEAD + state[0] * TAIL)

    def again(state):
        turn, out = state
        return turn + 1, out + run(turn[None])[0]

    return lax.while_loop(more, again, (jnp.int32(1), out))[1]


def solution(mesh):
    placed = (P("narrow", "wide", None), P())
    return jax.shard_map(
        shards, mesh=mesh, in_specs=placed, out_specs=P(("wide", "narrow"), None), check_vma=False
    )
```

```python
import functools

import jax
import jax.numpy as jnp
from jax import lax
from jax.experimental import pallas as pl
from jax.experimental.pallas import tpu as pltpu
from jax.sharding import PartitionSpec as P

MESH = pl.DeviceIdType.MESH
NX = NY = 4
NODES = NX * NY
EARLY, LATE = (5,), (4,)
STREAMS = EARLY + LATE
HEAD, TAIL = sum(EARLY), sum(LATE)
SLOTS = HEAD + TAIL
LANES = 128
STEP = 16.0
TOP = 32000.0
ROUTES = ("skip", 0), ("skip", 1)
STEPS = (0, (6, 3)), (1, (6, 3)), (0, (4, 1)), (1, (4, 1)), (0, (2,)), (1, (2,))
FIRST = (8, 7, 5), (8, 7, 5)
BALANCE, FIXES = 4, 6


def place():
    w = lax.axis_index("wide")
    return w // (2 * NX), lax.rem(w // 2, NX), lax.rem(w, 2)


def wide(y, x, q):
    return {"wide": (y * NX + x) * 2 + q}


NEAR = 10


def item(axis, distance, other):
    if distance == 0:
        return other
    if distance == 2:
        return NEAR + "xy".index(axis) * 2 + other
    return 2 + "xy".index(axis) * 4 + (distance - 1) + other


ITEMS = 2 * (NX + NY - 1)


def neighbours():
    y, x, q = place()
    return {
        ("x", 1): wide(y, lax.rem(x + 1, NX), q),
        ("x", -1): wide(y, lax.rem(x + NX - 1, NX), q),
        ("y", 1): wide(lax.rem(y + 1, NY), x, q),
        ("y", -1): wide(lax.rem(y + NY - 1, NY), x, q),
        ("x", 2): wide(y, lax.rem(x + 2, NX), q),
        ("y", 2): wide(lax.rem(y + 2, NY), x, q),
        "core": wide(y, x, 1 - q),
    }


def courier(view, pieces, send, recv):
    near = neighbours()
    started = []

    def both(src, dst, piece, to, sem):
        cut, at = pieces[piece]
        return pltpu.make_async_remote_copy(
            src_ref=view(src, cut),
            dst_ref=view(dst, cut),
            send_sem=send.at[sem],
            recv_sem=recv.at[dst, at],
            device_id=near[to],
            device_id_type=MESH,
        )

    def copy(src, dst, piece, to):
        c = both(src, dst, piece, to, len(started))
        c.start()
        started.append(c)

    def arrived(dst, piece):
        both(dst, dst, piece, "core", 0).wait_recv()

    def drain():
        for c in started:
            c.wait_send()

    return copy, arrived, drain


def gather_blocks(close, distant, send, recv):
    def view(k, cut):
        return close.at[(k,) + cut] if k < NEAR else distant.at[(k - NEAR,) + cut]

    copy, arrived, drain = courier(view, (((0,), 0), ((1,), 1)), send, recv)

    def start():
        for first in (0, 1):
            for a in "xy":
                copy(0, item(a, 3, 0), first, (a, 1))
                copy(0, item(a, 1, 0), 1 - first, (a, -1))
        for half in (0, 1):
            copy(0, 1, half, "core")

    def relay():
        for a in "xy":
            arrived(item(a, 3, 0), 0)
            copy(item(a, 3, 0), item(a, 2, 0), 0, (a, 1))
            arrived(item(a, 1, 0), 1)
            copy(item(a, 1, 0), item(a, 2, 0), 1, (a, -1))
        for a in "xy":
            copy(item(a, 3, 0), item(a, 3, 1), 0, "core")
            copy(item(a, 1, 0), item(a, 1, 1), 1, "core")

    def near():
        for a in "xy":
            arrived(item(a, 3, 0), 1)
            copy(item(a, 3, 0), item(a, 3, 1), 1, "core")
            arrived(item(a, 1, 0), 0)
            copy(item(a, 1, 0), item(a, 1, 1), 0, "core")
        for half in (0, 1):
            arrived(1, half)
            for a in "xy":
                arrived(item(a, 1, 1), half)
                arrived(item(a, 3, 1), half)

    def far():
        for half in (0, 1):
            for a in "xy":
                arrived(item(a, 2, 0), half)
                copy(item(a, 2, 0), item(a, 2, 1), half, "core")

    def finish():
        for half in (0, 1):
            for a in "xy":
                arrived(item(a, 2, 1), half)
        drain()

    return start, relay, near, far, finish


def exchange(buf, first, size, send, recv):
    cut = size // 2
    pieces = ((pl.ds(first, size),), 0), ((pl.ds(first, cut),), 0), ((pl.ds(first + cut, size - cut),), 1)
    copy, arrived, drain = courier(lambda k, cut: buf.at[(k,) + cut], pieces, send, recv)

    def start():
        for a in "xy":
            copy(0, item(a, 2, 0), 0, (a, 2))
        for a in "xy":
            copy(0, item(a, 3, 0), 0, (a, 1))
            copy(0, item(a, 1, 0), 0, (a, -1))
        copy(0, 1, 0, "core")

    def relay():
        for a in "xy":
            arrived(item(a, 3, 0), 0)
            copy(item(a, 3, 0), item(a, 3, 1), 0, "core")
            arrived(item(a, 1, 0), 0)
            copy(item(a, 1, 0), item(a, 1, 1), 0, "core")

    def far():
        for a in "xy":
            arrived(item(a, 2, 0), 0)
            copy(item(a, 2, 0), item(a, 2, 1), 0, "core")

    def finish():
        arrived(1, 0)
        for a in "xy":
            for d in (1, 3, 2):
                arrived(item(a, d, 1), 0)
        drain()

    return start, relay, far, finish


def encode(out, value):
    g = value.shape[0]
    rows = out.shape[1]
    halves = [value[:, :, :LANES], value[:, :, LANES:]]
    most = jnp.concatenate(
        [jnp.max(jnp.abs(h), axis=1) for h in halves] + [jnp.zeros((rows - 2 * g, LANES), jnp.float32)], axis=0
    )
    level = jnp.ceil(jnp.log2(jnp.maximum(most, 1e-30)) * STEP)
    out[2 * g] = level.astype(jnp.int32).astype(jnp.int16)
    inverse = jnp.exp2(level * (-1.0 / STEP)) * TOP
    for k in range(2):
        scaled = jnp.round(halves[k] * inverse[k * g : (k + 1) * g][:, None, :])
        out[k * g : (k + 1) * g] = scaled.astype(jnp.int32).astype(jnp.int16)


def scales(code):
    return jnp.exp2(code.astype(jnp.int32).astype(jnp.float32) * (1.0 / STEP)) * (1.0 / TOP)


def decode(ref):
    g = ref.shape[0] // 2
    scale = scales(ref[2 * g])
    tiles = ref[: 2 * g].astype(jnp.int32).astype(jnp.float32) * scale[: 2 * g][:, None, :]
    return jnp.concatenate([tiles[:g], tiles[g:]], axis=2)


def summed(value, axis):
    return jnp.sum(value, axis=axis, keepdims=True)


def balance(lo, hi, chosen):
    up = lax.broadcasted_iota(jnp.int32, (NODES, NODES), 0)
    across = lax.broadcasted_iota(jnp.int32, (NODES, NODES), 1)
    chip = lax.broadcasted_iota(jnp.int32, (NODES, lo.shape[1]), 0)
    is_lo = ((chip == lo) & chosen).astype(jnp.float32)
    is_hi = ((chip == hi) & chosen).astype(jnp.float32)
    lanes = (((1,), (1,)), ((), ()))
    count = lax.dot_general(is_lo, is_hi, lanes, preferred_element_type=jnp.float32)
    count += lax.dot_general(is_hi, is_lo, lanes, preferred_element_type=jnp.float32)
    same = up == across
    loops = jnp.where(same, count * 0.5, 0.0)
    count = jnp.where(same, 0.0, count)
    loops_up, loops_across = summed(loops, 1), summed(loops, 0)

    def loads(give):
        return summed(give, 1) + loops_up, summed(count - give, 0) + loops_across

    give = count * 0.5
    for _ in range(BALANCE):
        load_up, load_across = loads(give)
        give = jnp.clip(give - (load_up - load_across) * (1.0 / NODES), 0.0, count)
    give = jnp.where(up < across, jnp.floor(give + 0.5), count - jnp.floor(count - give + 0.5))
    tag_up, tag_across = up.astype(jnp.float32), across.astype(jnp.float32)
    for _ in range(FIXES):
        load_up, load_across = loads(give)
        full_up, full_across = load_up * 64.0 + tag_up, load_across * 64.0 + tag_across
        full = jnp.max(jnp.max(full_across, axis=1, keepdims=True), axis=0, keepdims=True)
        target = jnp.where((full_up == full) & (give > 0.0), full_across, 1e9)
        mirror = jnp.where((full_across == full) & (count - give > 0.0), full_up, 1e9)
        least = jnp.min(jnp.min(target, axis=1, keepdims=True), axis=0, keepdims=True)
        move = (full - least >= 128.0).astype(jnp.float32)
        give = give - jnp.where(target == least, move, 0.0) + jnp.where(mirror == least, move, 0.0)
    share = lax.dot_general(give, is_lo, (((0,), (0,)), ((), ())), preferred_element_type=jnp.float32)
    return summed(share * is_hi, 0)


def tables(pairs, turn):
    y, x, q = place()
    n = pairs.shape[1]
    up = lax.broadcasted_iota(jnp.int32, (n, n), 0)
    across = lax.broadcasted_iota(jnp.int32, (n, n), 1)
    same, before = up == across, up < across

    def column(v):
        return summed(jnp.where(same, v, 0), 1)

    def ranks(key):
        return summed(jnp.where((column(key) == key) & before, 1, 0), 0)

    r, c = pairs[0:1, :], pairs[1:2, :]
    yr, xr, yc, xc = r >> 3, (r >> 1) & 3, c >> 3, (c >> 1) & 3
    far_x, far_y = ((xr - xc) & 3) == 2, ((yr - yc) & 3) == 2
    middle_x, middle_y = far_x & (yr == yc), far_y & (xr == xc)
    late = (far_x | far_y) & jnp.logical_not(middle_x | middle_y)
    kind = late.astype(jnp.int32)
    one, two = yr * NX + xc, yc * NX + xr
    one = jnp.where(middle_x, yr * NX + ((xr + 1) & 3), jnp.where(middle_y, ((yr + 1) & 3) * NX + xr, one))
    two = jnp.where(middle_x, yr * NX + ((xr + 3) & 3), jnp.where(middle_y, ((yr + 3) & 3) * NX + xr, two))
    lo, hi = jnp.minimum(one, two), jnp.maximum(one, two)
    share = jnp.where(late, balance(lo, hi, late), balance(lo, hi, jnp.logical_not(late)))
    rank = ranks((lo * NODES + hi) * 2 + kind)
    node = jnp.where(rank.astype(jnp.float32) < share, lo, hi)
    rank = ranks(node * 2 + kind)
    node_up = column(node)
    ahead = summed(jnp.where((node_up == node) & (column(kind) == 0), 1, 0), 0)
    rank = jnp.where(late, jnp.maximum(ahead, 2 * HEAD) + rank, rank)
    most = jnp.broadcast_to(jnp.max(rank, axis=1, keepdims=True) + 1, (1, LANES))

    r, c, node, rank = column(r), column(c), node_up, column(rank)
    core, slot = rank & 1, (rank >> 1) - turn * TAIL
    inside = (slot >= jnp.where(turn > 0, HEAD, 0)) & (slot < SLOTS)
    lane = lax.broadcasted_iota(jnp.int32, (r.shape[0], LANES), 1)

    def seen(block_y, block_x, other):
        aside = block_y != y
        d = jnp.where(aside, block_y - y, block_x - x) & 3
        line = aside.astype(jnp.int32)
        return other + jnp.where(d == 0, 0, jnp.where(d == 2, NEAR + 2 * line, 1 + 4 * line + d))

    pick = (node == y * NX + x) & (core == q) & inside & (slot == lane)
    rows = summed(jnp.where(pick, seen(r >> 3, (r >> 1) & 3, (r & 1) ^ q), 0), 0)
    cols = summed(jnp.where(pick, seen(c >> 3, (c >> 1) & 3, (c & 1) ^ q), 0), 0)
    want = (r == (y * NX + x) * 2 + q) & inside & (c == lane)
    src = summed(jnp.where(want, seen(node >> 2, node & 3, core ^ q), 0), 0)
    at = summed(jnp.where(want, slot, 0), 0)
    live = summed(jnp.where(want, 1, 0), 0)
    rows, cols, src = [jnp.minimum(v, ITEMS - 1) for v in (rows, cols, src)]
    return rows, cols, src, jnp.minimum(at, SLOTS - 1), live, most


PARENTS = {
    "ring": {k: k - 1 for k in range(1, 9)},
    "skip": {8: 6, 7: 6, 6: 4, 5: 4, 4: 2, 3: 2, 2: 0, 1: 0},
    "mix": {8: 6, 7: 6, 6: 4, 5: 4, 4: 2, 3: 2, 2: 1, 1: 0},
}


def trees(group):
    pattern, longer = ROUTES[group]
    return [{k: p for k, p in PARENTS[pattern].items() if k < 8 or side == longer} for side in (0, 1)]


def kernel(
    nz, turn, pairs, factors, out, most_out, close, distant, partial, z_out, z_in, parts, scale, table, table_s,
    listed, listed_sem, local, gsend, grecv, zsend, zrecv, xsend, xrecv,
):
    z = lax.axis_index("narrow")
    rows = close.shape[2]
    chunk = rows // nz
    forest = [trees(0)] * len(EARLY) + [trees(1)] * len(LATE)
    starts = [sum(STREAMS[:s]) for s in range(len(STREAMS))]

    def away(d):
        return {"narrow": lax.rem(z + d + nz, nz)}

    own = pltpu.make_async_copy(factors, close.at[0], local)
    own.start()
    listing = pltpu.make_async_copy(pairs, listed, listed_sem)
    listing.start()
    barrier = pltpu.get_barrier_semaphore()
    hops = sorted({sign * (k - p) for trees in forest for t in trees for k, p in t.items() for sign in (1, -1)})
    peers = list(neighbours().values()) + [away(d) for d in hops]
    for peer in peers:
        pl.semaphore_signal(barrier, inc=1, device_id=peer, device_id_type=MESH)
    own.wait()
    listing.wait()
    pl.semaphore_wait(barrier, len(peers))

    start, relay, near, far, finish = gather_blocks(close, distant, gsend, grecv)
    start()
    for k, v in enumerate(tables(listed[...], turn[0])):
        table[k : k + 1, :] = v
    scalars = pltpu.make_async_copy(table, table_s, local)
    scalars.start()
    relay()
    scalars.wait()
    most_out[0] = table_s[5, 0]

    def tile(s, load):
        i, j = table_s[0, s], table_s[1, s]
        contract = (((1,), (1,)), ((), ()))
        partial[s] = sum(
            lax.dot_general(load(i, p), load(j, p), contract, preferred_element_type=jnp.float32) for p in (0, 1)
        )

    def load_close(i, p):
        return close[jnp.minimum(i, NEAR - 1), p]

    def load_any(i, p):
        return jnp.where(i < NEAR, load_close(i, p), distant[jnp.maximum(i - NEAR, 0), p])

    def span(stream):
        at = 2 * starts[stream] + stream
        return pl.ds(at, 2 * STREAMS[stream] + 1)

    def mine(dest, stream):
        at = pl.multiple_of(dest * chunk, chunk)
        return partial[pl.ds(starts[stream], STREAMS[stream]), pl.ds(at, chunk), :]

    def hop(side, k, stream):
        buf = side * (nz // 2) + k - 1
        return pltpu.make_async_remote_copy(
            src_ref=z_out.at[buf, span(stream)],
            dst_ref=z_in.at[buf, span(stream)],
            send_sem=zsend.at[buf, stream],
            recv_sem=zrecv.at[buf, stream],
            device_id=away((1, -1)[side] * (k - forest[stream][side][k])),
            device_id_type=MESH,
        )

    sent = []

    def gathered(side, k, stream, value):
        for child, parent in sorted(forest[stream][side].items(), reverse=True):
            if parent == k:
                hop(side, child, stream).wait_recv()
                value += decode(z_in.at[side * (nz // 2) + child - 1, span(stream)])
        return value

    def send(side, k, stream):
        dest = lax.rem(z + (1, -1)[side] * k + nz, nz)
        value = gathered(side, k, stream, mine(dest, stream))
        encode(z_out.at[side * (nz // 2) + k - 1, span(stream)], value)
        c = hop(side, k, stream)
        c.start()
        sent.append(c)

    def leg(ks, streams):
        for stream in streams:
            for k in ks:
                for side in (0, 1):
                    if k in forest[stream][side]:
                        send(side, k, stream)

    def make(streams, load):
        def one(s, _):
            tile(s, load)
            return 0

        for stream in streams:
            lax.fori_loop(starts[stream], starts[stream] + STREAMS[stream], one, 0)

    groups = (range(len(EARLY)), range(len(EARLY), len(STREAMS)))
    near()
    make(groups[0], load_close)
    leg(FIRST[0], groups[0])
    far()
    leg((6,), groups[0])
    finish()
    make(groups[1], load_any)
    leg(FIRST[1], groups[1])
    leg((3,), groups[0])
    for group, ks in STEPS[1:]:
        leg(ks, groups[group])
    swaps = []
    for stream, g in enumerate(STREAMS):
        value = mine(z, stream)
        for side in (1, 0):
            value = gathered(side, 0, stream, value)
        encode(parts.at[0, span(stream)], value)
        swaps.append(exchange(parts, 2 * starts[stream] + stream, 2 * g + 1, xsend.at[stream], xrecv.at[stream]))
        swaps[-1][0]()
    for swap in swaps:
        swap[1]()
    for swap in swaps:
        swap[2]()
    for swap in swaps:
        swap[3]()
    for k in range(ITEMS):
        for stream, g in enumerate(STREAMS):
            s = scales(parts[k, 2 * starts[stream] + stream + 2 * g])
            for j in range(g):
                scale[k * SLOTS + starts[stream] + j, 0:1, :] = s[j : j + 1]
                scale[k * SLOTS + starts[stream] + j, 1:2, :] = s[g + j : g + j + 1]
    nblk = out.shape[1] // rows
    for c in range(nblk):
        src, slot, live = table_s[2, c], table_s[3, c], table_s[4, c]
        first, step = slot, STREAMS[0]
        for stream in range(1, len(STREAMS)):
            later = slot >= starts[stream]
            first = jnp.where(later, slot + starts[stream] + stream, first)
            step = jnp.where(later, STREAMS[stream], step)
        s = scale[src * SLOTS + slot]
        for h in range(2):
            found = parts[src, first + h * step].astype(jnp.int32).astype(jnp.float32) * s[h : h + 1]
            out[:, c * rows + h * LANES : c * rows + (h + 1) * LANES] = jnp.where(live > 0, found, 0.0)
    for c in sent:
        c.wait_send()


def shards(factors, pairs):
    nz = lax.axis_size("narrow")
    two, rows, occ = factors.shape
    nblk = lax.axis_size("wide")
    chunk = rows // nz
    tiles = 2 * SLOTS + len(STREAMS)
    hops = (nz, len(STREAMS))
    pairs = pairs.T

    def run(turn):
        return pl.pallas_call(
            functools.partial(kernel, nz),
            out_shape=(
                jax.ShapeDtypeStruct((chunk, nblk * rows), jnp.float32),
                jax.ShapeDtypeStruct((1,), jnp.int32),
            ),
            in_specs=[
                pl.BlockSpec(memory_space=pltpu.SMEM),
                pl.BlockSpec(memory_space=pl.ANY),
                pl.BlockSpec(memory_space=pl.ANY),
            ],
            out_specs=[pl.BlockSpec(memory_space=pltpu.VMEM), pl.BlockSpec(memory_space=pltpu.SMEM)],
            scratch_shapes=[
                pltpu.VMEM((NEAR, two, rows, occ), jnp.bfloat16),
                pltpu.VMEM((ITEMS - NEAR, two, rows, occ), jnp.bfloat16),
                pltpu.VMEM((SLOTS, rows, rows), jnp.float32),
                pltpu.VMEM((nz, tiles, chunk, LANES), jnp.int16),
                pltpu.VMEM((nz, tiles, chunk, LANES), jnp.int16),
                pltpu.VMEM((ITEMS, tiles, chunk, LANES), jnp.int16),
                pltpu.VMEM((ITEMS * SLOTS, 8, LANES), jnp.float32),
                pltpu.VMEM((8, LANES), jnp.int32),
                pltpu.SMEM((8, LANES), jnp.int32),
                pltpu.VMEM(pairs.shape, jnp.int32),
                pltpu.SemaphoreType.DMA,
                pltpu.SemaphoreType.DMA,
                pltpu.SemaphoreType.DMA((2 * ITEMS - 2,)),
                pltpu.SemaphoreType.DMA((ITEMS, 2)),
                pltpu.SemaphoreType.DMA(hops),
                pltpu.SemaphoreType.DMA(hops),
                pltpu.SemaphoreType.DMA((len(STREAMS), 15)),
                pltpu.SemaphoreType.DMA((len(STREAMS), ITEMS, 2)),
            ],
            compiler_params=pltpu.CompilerParams(
                collective_id=0, has_side_effects=True, vmem_limit_bytes=48 * 1024 * 1024
            ),
        )(turn, pairs, factors)

    out, most = run(jnp.zeros((1,), jnp.int32))

    def more(state):
        return most[0] > 2 * (HEAD + state[0] * TAIL)

    def again(state):
        turn, out = state
        return turn + 1, out + run(turn[None])[0]

    def rest(out):
        return lax.while_loop(more, again, (jnp.int32(1), out))[1]

    return lax.cond(most[0] > 2 * SLOTS, rest, lambda out: out, out)


def solution(mesh):
    placed = (P("narrow", "wide", None), P())
    return jax.shard_map(
        shards, mesh=mesh, in_specs=placed, out_specs=P(("wide", "narrow"), None), check_vma=False
    )
```

```python
import functools

import jax
import jax.numpy as jnp
from jax import lax
from jax.experimental import pallas as pl
from jax.experimental.pallas import tpu as pltpu
from jax.sharding import PartitionSpec as P

MESH = pl.DeviceIdType.MESH
NX = NY = 4
NODES = NX * NY
EARLY, LATE = (5,), (4,)
STREAMS = EARLY + LATE
HEAD, TAIL = sum(EARLY), sum(LATE)
SLOTS = HEAD + TAIL
LANES = 128
STEP = 16.0
TOP = 32000.0
ROUTES = ("skip", 0), ("skip", 1)
STEPS = (0, (6, 3)), (1, (6, 3)), (0, (4, 1)), (1, (4, 1)), (0, (2,)), (1, (2,))
FIRST = (8, 7, 5), (8, 7, 5)
BALANCE, FIXES = 4, 6


def place():
    w = lax.axis_index("wide")
    return w // (2 * NX), lax.rem(w // 2, NX), lax.rem(w, 2)


def wide(y, x, q):
    return {"wide": (y * NX + x) * 2 + q}


NEAR = 10


def item(axis, distance, other):
    if distance == 0:
        return other
    if distance == 2:
        return NEAR + "xy".index(axis) * 2 + other
    return 2 + "xy".index(axis) * 4 + (distance - 1) + other


ITEMS = 2 * (NX + NY - 1)


def neighbours():
    y, x, q = place()
    return {
        ("x", 1): wide(y, lax.rem(x + 1, NX), q),
        ("x", -1): wide(y, lax.rem(x + NX - 1, NX), q),
        ("y", 1): wide(lax.rem(y + 1, NY), x, q),
        ("y", -1): wide(lax.rem(y + NY - 1, NY), x, q),
        ("x", 2): wide(y, lax.rem(x + 2, NX), q),
        ("y", 2): wide(lax.rem(y + 2, NY), x, q),
        "core": wide(y, x, 1 - q),
    }


def courier(view, pieces, send, recv):
    near = neighbours()
    started = []

    def both(src, dst, piece, to, sem, origin=None):
        cut, at = pieces[piece]
        return pltpu.make_async_remote_copy(
            src_ref=view(src, cut) if origin is None else origin.at[cut],
            dst_ref=view(dst, cut),
            send_sem=send.at[sem],
            recv_sem=recv.at[dst, at],
            device_id=near[to],
            device_id_type=MESH,
        )

    def copy(src, dst, piece, to, origin=None):
        c = both(src, dst, piece, to, len(started), origin)
        c.start()
        started.append(c)

    def arrived(dst, piece):
        both(dst, dst, piece, "core", 0).wait_recv()

    def drain():
        for c in started:
            c.wait_send()

    return copy, arrived, drain


def gather_blocks(own, close, distant, send, recv):
    def view(k, cut):
        return close.at[(k,) + cut] if k < NEAR else distant.at[(k - NEAR,) + cut]

    copy, arrived, drain = courier(view, (((0,), 0), ((1,), 1)), send, recv)

    def start():
        for first in (0, 1):
            for a in "xy":
                copy(0, item(a, 3, 0), first, (a, 1), own)
                copy(0, item(a, 1, 0), 1 - first, (a, -1), own)
        for half in (0, 1):
            copy(0, 1, half, "core", own)

    def relay():
        for a in "xy":
            arrived(item(a, 3, 0), 0)
            copy(item(a, 3, 0), item(a, 2, 0), 0, (a, 1))
            arrived(item(a, 1, 0), 1)
            copy(item(a, 1, 0), item(a, 2, 0), 1, (a, -1))
        for a in "xy":
            copy(item(a, 3, 0), item(a, 3, 1), 0, "core")
            copy(item(a, 1, 0), item(a, 1, 1), 1, "core")

    def near():
        for a in "xy":
            arrived(item(a, 3, 0), 1)
            copy(item(a, 3, 0), item(a, 3, 1), 1, "core")
            arrived(item(a, 1, 0), 0)
            copy(item(a, 1, 0), item(a, 1, 1), 0, "core")
        for half in (0, 1):
            arrived(1, half)
            for a in "xy":
                arrived(item(a, 1, 1), half)
                arrived(item(a, 3, 1), half)

    def far():
        for half in (0, 1):
            for a in "xy":
                arrived(item(a, 2, 0), half)
                copy(item(a, 2, 0), item(a, 2, 1), half, "core")

    def finish():
        for half in (0, 1):
            for a in "xy":
                arrived(item(a, 2, 1), half)
        drain()

    return start, relay, near, far, finish


def exchange(buf, first, size, send, recv):
    cut = size // 2
    pieces = ((pl.ds(first, size),), 0), ((pl.ds(first, cut),), 0), ((pl.ds(first + cut, size - cut),), 1)
    copy, arrived, drain = courier(lambda k, cut: buf.at[(k,) + cut], pieces, send, recv)

    def start():
        for a in "xy":
            copy(0, item(a, 2, 0), 0, (a, 2))
        for a in "xy":
            copy(0, item(a, 3, 0), 0, (a, 1))
            copy(0, item(a, 1, 0), 0, (a, -1))
        copy(0, 1, 0, "core")

    def relay():
        for a in "xy":
            arrived(item(a, 3, 0), 0)
            copy(item(a, 3, 0), item(a, 3, 1), 0, "core")
            arrived(item(a, 1, 0), 0)
            copy(item(a, 1, 0), item(a, 1, 1), 0, "core")

    def far():
        for a in "xy":
            arrived(item(a, 2, 0), 0)
            copy(item(a, 2, 0), item(a, 2, 1), 0, "core")

    def finish():
        arrived(1, 0)
        for a in "xy":
            for d in (1, 3, 2):
                arrived(item(a, d, 1), 0)
        drain()

    return start, relay, far, finish


def encode(out, value):
    g = value.shape[0]
    rows = out.shape[1]
    halves = [value[:, :, :LANES], value[:, :, LANES:]]
    most = jnp.concatenate(
        [jnp.max(jnp.abs(h), axis=1) for h in halves] + [jnp.zeros((rows - 2 * g, LANES), jnp.float32)], axis=0
    )
    level = jnp.ceil(jnp.log2(jnp.maximum(most, 1e-30)) * STEP)
    out[2 * g] = level.astype(jnp.int32).astype(jnp.int16)
    inverse = jnp.exp2(level * (-1.0 / STEP)) * TOP
    for k in range(2):
        scaled = jnp.round(halves[k] * inverse[k * g : (k + 1) * g][:, None, :])
        out[k * g : (k + 1) * g] = scaled.astype(jnp.int32).astype(jnp.int16)


def scales(code):
    return jnp.exp2(code.astype(jnp.int32).astype(jnp.float32) * (1.0 / STEP)) * (1.0 / TOP)


def decode(ref):
    g = ref.shape[0] // 2
    scale = scales(ref[2 * g])
    tiles = ref[: 2 * g].astype(jnp.int32).astype(jnp.float32) * scale[: 2 * g][:, None, :]
    return jnp.concatenate([tiles[:g], tiles[g:]], axis=2)


def summed(value, axis):
    return jnp.sum(value, axis=axis, keepdims=True)


def balance(lo, hi, chosen):
    up = lax.broadcasted_iota(jnp.int32, (NODES, NODES), 0)
    across = lax.broadcasted_iota(jnp.int32, (NODES, NODES), 1)
    chip = lax.broadcasted_iota(jnp.int32, (NODES, lo.shape[1]), 0)
    is_lo = ((chip == lo) & chosen).astype(jnp.float32)
    is_hi = ((chip == hi) & chosen).astype(jnp.float32)
    lanes = (((1,), (1,)), ((), ()))
    count = lax.dot_general(is_lo, is_hi, lanes, preferred_element_type=jnp.float32)
    count += lax.dot_general(is_hi, is_lo, lanes, preferred_element_type=jnp.float32)
    same = up == across
    loops = jnp.where(same, count * 0.5, 0.0)
    count = jnp.where(same, 0.0, count)
    loops_up, loops_across = summed(loops, 1), summed(loops, 0)

    def loads(give):
        return summed(give, 1) + loops_up, summed(count - give, 0) + loops_across

    give = count * 0.5
    for _ in range(BALANCE):
        load_up, load_across = loads(give)
        give = jnp.clip(give - (load_up - load_across) * (1.0 / NODES), 0.0, count)
    give = jnp.where(up < across, jnp.floor(give + 0.5), count - jnp.floor(count - give + 0.5))
    tag_up, tag_across = up.astype(jnp.float32), across.astype(jnp.float32)
    for _ in range(FIXES):
        load_up, load_across = loads(give)
        full_up, full_across = load_up * 64.0 + tag_up, load_across * 64.0 + tag_across
        full = jnp.max(jnp.max(full_across, axis=1, keepdims=True), axis=0, keepdims=True)
        target = jnp.where((full_up == full) & (give > 0.0), full_across, 1e9)
        mirror = jnp.where((full_across == full) & (count - give > 0.0), full_up, 1e9)
        least = jnp.min(jnp.min(target, axis=1, keepdims=True), axis=0, keepdims=True)
        move = (full - least >= 128.0).astype(jnp.float32)
        give = give - jnp.where(target == least, move, 0.0) + jnp.where(mirror == least, move, 0.0)
    share = lax.dot_general(give, is_lo, (((0,), (0,)), ((), ())), preferred_element_type=jnp.float32)
    return summed(share * is_hi, 0)


def tables(pairs, turn):
    y, x, q = place()
    n = pairs.shape[1]
    up = lax.broadcasted_iota(jnp.int32, (n, n), 0)
    across = lax.broadcasted_iota(jnp.int32, (n, n), 1)
    same, before = up == across, up < across

    def column(v):
        return summed(jnp.where(same, v, 0), 1)

    def ranks(key):
        return summed(jnp.where((column(key) == key) & before, 1, 0), 0)

    r, c = pairs[0:1, :], pairs[1:2, :]
    yr, xr, yc, xc = r >> 3, (r >> 1) & 3, c >> 3, (c >> 1) & 3
    far_x, far_y = ((xr - xc) & 3) == 2, ((yr - yc) & 3) == 2
    middle_x, middle_y = far_x & (yr == yc), far_y & (xr == xc)
    late = (far_x | far_y) & jnp.logical_not(middle_x | middle_y)
    kind = late.astype(jnp.int32)
    one, two = yr * NX + xc, yc * NX + xr
    one = jnp.where(middle_x, yr * NX + ((xr + 1) & 3), jnp.where(middle_y, ((yr + 1) & 3) * NX + xr, one))
    two = jnp.where(middle_x, yr * NX + ((xr + 3) & 3), jnp.where(middle_y, ((yr + 3) & 3) * NX + xr, two))
    lo, hi = jnp.minimum(one, two), jnp.maximum(one, two)
    share = jnp.where(late, balance(lo, hi, late), balance(lo, hi, jnp.logical_not(late)))
    rank = ranks((lo * NODES + hi) * 2 + kind)
    node = jnp.where(rank.astype(jnp.float32) < share, lo, hi)
    rank = ranks(node * 2 + kind)
    node_up = column(node)
    ahead = summed(jnp.where((node_up == node) & (column(kind) == 0), 1, 0), 0)
    rank = jnp.where(late, jnp.maximum(ahead, 2 * HEAD) + rank, rank)
    most = jnp.broadcast_to(jnp.max(rank, axis=1, keepdims=True) + 1, (1, LANES))

    r, c, node, rank = column(r), column(c), node_up, column(rank)
    core, slot = rank & 1, (rank >> 1) - turn * TAIL
    inside = (slot >= jnp.where(turn > 0, HEAD, 0)) & (slot < SLOTS)
    lane = lax.broadcasted_iota(jnp.int32, (r.shape[0], LANES), 1)

    def seen(block_y, block_x, other):
        aside = block_y != y
        d = jnp.where(aside, block_y - y, block_x - x) & 3
        line = aside.astype(jnp.int32)
        return other + jnp.where(d == 0, 0, jnp.where(d == 2, NEAR + 2 * line, 1 + 4 * line + d))

    pick = (node == y * NX + x) & (core == q) & inside & (slot == lane)
    rows = summed(jnp.where(pick, seen(r >> 3, (r >> 1) & 3, (r & 1) ^ q), 0), 0)
    cols = summed(jnp.where(pick, seen(c >> 3, (c >> 1) & 3, (c & 1) ^ q), 0), 0)
    want = (r == (y * NX + x) * 2 + q) & inside & (c == lane)
    src = summed(jnp.where(want, seen(node >> 2, node & 3, core ^ q), 0), 0)
    at = summed(jnp.where(want, slot, 0), 0)
    live = summed(jnp.where(want, 1, 0), 0)
    rows, cols, src = [jnp.minimum(v, ITEMS - 1) for v in (rows, cols, src)]
    return rows, cols, src, jnp.minimum(at, SLOTS - 1), live, most


PARENTS = {
    "ring": {k: k - 1 for k in range(1, 9)},
    "skip": {8: 6, 7: 6, 6: 4, 5: 4, 4: 2, 3: 2, 2: 0, 1: 0},
    "mix": {8: 6, 7: 6, 6: 4, 5: 4, 4: 2, 3: 2, 2: 1, 1: 0},
}


def trees(group):
    pattern, longer = ROUTES[group]
    return [{k: p for k, p in PARENTS[pattern].items() if k < 8 or side == longer} for side in (0, 1)]


def kernel(
    nz, turn, pairs, factors, out, again_out, echo, close, distant, partial, z_out, z_in, parts, scale, table, table_s,
    listed, listed_sem, local, gsend, grecv, zsend, zrecv, xsend, xrecv,
):
    z = lax.axis_index("narrow")
    rows = close.shape[2]
    chunk = rows // nz
    forest = [trees(0)] * len(EARLY) + [trees(1)] * len(LATE)
    starts = [sum(STREAMS[:s]) for s in range(len(STREAMS))]

    def away(d):
        return {"narrow": lax.rem(z + d + nz, nz)}

    own = pltpu.make_async_copy(factors, close.at[0], local)
    own.start()
    listing = pltpu.make_async_copy(pairs, listed, listed_sem)
    listing.start()
    barrier = pltpu.get_barrier_semaphore()
    hops = sorted({sign * (k - p) for trees in forest for t in trees for k, p in t.items() for sign in (1, -1)})
    peers = list(neighbours().values()) + [away(d) for d in hops]
    for peer in peers:
        pl.semaphore_signal(barrier, inc=1, device_id=peer, device_id_type=MESH)
    pl.semaphore_wait(barrier, len(peers))

    start, relay, near, far, finish = gather_blocks(factors, close, distant, gsend, grecv)
    start()
    listing.wait()
    own.wait()
    for k, v in enumerate(tables(listed[...], turn[0])):
        table[k : k + 1, :] = v
    scalars = pltpu.make_async_copy(table, table_s, local)
    scalars.start()
    relay()
    scalars.wait()
    again_out[0] = jnp.where(table_s[5, 0] > 2 * (HEAD + (turn[0] + 1) * TAIL), 1, 0)
    echo[...] = listed[...]

    def tile(s, load):
        i, j = table_s[0, s], table_s[1, s]
        contract = (((1,), (1,)), ((), ()))
        partial[s] = sum(
            lax.dot_general(load(i, p), load(j, p), contract, preferred_element_type=jnp.float32) for p in (0, 1)
        )

    def load_close(i, p):
        return close[jnp.minimum(i, NEAR - 1), p]

    def load_any(i, p):
        return jnp.where(i < NEAR, load_close(i, p), distant[jnp.maximum(i - NEAR, 0), p])

    def span(stream):
        at = 2 * starts[stream] + stream
        return pl.ds(at, 2 * STREAMS[stream] + 1)

    def mine(dest, stream):
        at = pl.multiple_of(dest * chunk, chunk)
        return partial[pl.ds(starts[stream], STREAMS[stream]), pl.ds(at, chunk), :]

    def hop(side, k, stream):
        buf = side * (nz // 2) + k - 1
        return pltpu.make_async_remote_copy(
            src_ref=z_out.at[buf, span(stream)],
            dst_ref=z_in.at[buf, span(stream)],
            send_sem=zsend.at[buf, stream],
            recv_sem=zrecv.at[buf, stream],
            device_id=away((1, -1)[side] * (k - forest[stream][side][k])),
            device_id_type=MESH,
        )

    sent = []

    def gathered(side, k, stream, value):
        for child, parent in sorted(forest[stream][side].items(), reverse=True):
            if parent == k:
                hop(side, child, stream).wait_recv()
                value += decode(z_in.at[side * (nz // 2) + child - 1, span(stream)])
        return value

    def send(side, k, stream):
        dest = lax.rem(z + (1, -1)[side] * k + nz, nz)
        value = gathered(side, k, stream, mine(dest, stream))
        encode(z_out.at[side * (nz // 2) + k - 1, span(stream)], value)
        c = hop(side, k, stream)
        c.start()
        sent.append(c)

    def leg(ks, streams):
        for stream in streams:
            for k in ks:
                for side in (0, 1):
                    if k in forest[stream][side]:
                        send(side, k, stream)

    def make(streams, load):
        def one(s, _):
            tile(s, load)
            return 0

        for stream in streams:
            lax.fori_loop(starts[stream], starts[stream] + STREAMS[stream], one, 0)

    groups = (range(len(EARLY)), range(len(EARLY), len(STREAMS)))
    near()
    make(groups[0], load_close)
    leg(FIRST[0], groups[0])
    far()
    leg((6,), groups[0])
    finish()
    make(groups[1], load_any)
    leg(FIRST[1], groups[1])
    leg((3,), groups[0])
    for group, ks in STEPS[1:]:
        leg(ks, groups[group])
    swaps = []
    for stream, g in enumerate(STREAMS):
        value = mine(z, stream)
        for side in (1, 0):
            value = gathered(side, 0, stream, value)
        encode(parts.at[0, span(stream)], value)
        swaps.append(exchange(parts, 2 * starts[stream] + stream, 2 * g + 1, xsend.at[stream], xrecv.at[stream]))
        swaps[-1][0]()
    for swap in swaps:
        swap[1]()
    for swap in swaps:
        swap[2]()
    for swap in swaps:
        swap[3]()
    for k in range(ITEMS):
        for stream, g in enumerate(STREAMS):
            s = scales(parts[k, 2 * starts[stream] + stream + 2 * g])
            for j in range(g):
                scale[k * SLOTS + starts[stream] + j, 0:1, :] = s[j : j + 1]
                scale[k * SLOTS + starts[stream] + j, 1:2, :] = s[g + j : g + j + 1]
    nblk = out.shape[1] // rows
    for c in range(nblk):
        src, slot, live = table_s[2, c], table_s[3, c], table_s[4, c]
        first, step = slot, STREAMS[0]
        for stream in range(1, len(STREAMS)):
            later = slot >= starts[stream]
            first = jnp.where(later, slot + starts[stream] + stream, first)
            step = jnp.where(later, STREAMS[stream], step)
        s = scale[src * SLOTS + slot]
        for h in range(2):
            found = parts[src, first + h * step].astype(jnp.int32).astype(jnp.float32) * s[h : h + 1]
            out[:, c * rows + h * LANES : c * rows + (h + 1) * LANES] = jnp.where(live > 0, found, 0.0)
    for c in sent:
        c.wait_send()


def shards(factors, pairs):
    nz = lax.axis_size("narrow")
    two, rows, occ = factors.shape
    nblk = lax.axis_size("wide")
    chunk = rows // nz
    tiles = 2 * SLOTS + len(STREAMS)
    hops = (nz, len(STREAMS))
    pairs = pairs.T

    def run(pairs, turn):
        return pl.pallas_call(
            functools.partial(kernel, nz),
            out_shape=(
                jax.ShapeDtypeStruct((chunk, nblk * rows), jnp.float32),
                jax.ShapeDtypeStruct((1,), jnp.int32),
                jax.ShapeDtypeStruct(pairs.shape, jnp.int32),
            ),
            in_specs=[
                pl.BlockSpec(memory_space=pltpu.SMEM),
                pl.BlockSpec(memory_space=pl.ANY),
                pl.BlockSpec(memory_space=pl.ANY),
            ],
            out_specs=[
                pl.BlockSpec(memory_space=pltpu.VMEM),
                pl.BlockSpec(memory_space=pltpu.SMEM),
                pl.BlockSpec(memory_space=pltpu.VMEM),
            ],
            scratch_shapes=[
                pltpu.VMEM((NEAR, two, rows, occ), jnp.bfloat16),
                pltpu.VMEM((ITEMS - NEAR, two, rows, occ), jnp.bfloat16),
                pltpu.VMEM((SLOTS, rows, rows), jnp.float32),
                pltpu.VMEM((nz, tiles, chunk, LANES), jnp.int16),
                pltpu.VMEM((nz, tiles, chunk, LANES), jnp.int16),
                pltpu.VMEM((ITEMS, tiles, chunk, LANES), jnp.int16),
                pltpu.VMEM((ITEMS * SLOTS, 8, LANES), jnp.float32),
                pltpu.VMEM((8, LANES), jnp.int32),
                pltpu.SMEM((8, LANES), jnp.int32),
                pltpu.VMEM(pairs.shape, jnp.int32),
                pltpu.SemaphoreType.DMA,
                pltpu.SemaphoreType.DMA,
                pltpu.SemaphoreType.DMA((2 * ITEMS - 2,)),
                pltpu.SemaphoreType.DMA((ITEMS, 2)),
                pltpu.SemaphoreType.DMA(hops),
                pltpu.SemaphoreType.DMA(hops),
                pltpu.SemaphoreType.DMA((len(STREAMS), 15)),
                pltpu.SemaphoreType.DMA((len(STREAMS), ITEMS, 2)),
            ],
            compiler_params=pltpu.CompilerParams(
                collective_id=0, has_side_effects=True, vmem_limit_bytes=62 * 1024 * 1024
            ),
        )(turn, pairs, factors)

    out, more, pairs = run(pairs, jnp.zeros((1,), jnp.int32))

    def rest(pairs, out):
        def again(state):
            turn, out, _, pairs = state
            further, more, pairs = run(pairs, turn[None])
            return turn + 1, out + further, more, pairs

        state = (jnp.int32(1), out, jnp.ones((1,), jnp.int32), pairs)
        return lax.while_loop(lambda state: state[2][0] > 0, again, state)[1]

    return lax.switch(more[0], [lambda pairs, out: out, rest], pairs, out)


def solution(mesh):
    placed = (P("narrow", "wide", None), P())
    return jax.shard_map(
        shards, mesh=mesh, in_specs=placed, out_specs=P(("wide", "narrow"), None), check_vma=False
    )
```

```python
import functools

import jax
import jax.numpy as jnp
from jax import lax
from jax.experimental import pallas as pl
from jax.experimental.pallas import tpu as pltpu
from jax.sharding import PartitionSpec as P

MESH = pl.DeviceIdType.MESH
NX = NY = 4
NODES = NX * NY
EARLY, LATE = (5,), (4,)
STREAMS = EARLY + LATE
HEAD, TAIL = sum(EARLY), sum(LATE)
SLOTS = HEAD + TAIL
LANES = 128
STEP = 16.0
TOP = 32000.0
ROUTES = ("skip", 0), ("skip", 1)
STEPS = (0, (6, 3)), (1, (6,)), (0, (4,)), (1, (3,)), (0, (1,)), (1, (4, 1)), (0, (2,)), (1, (2,))
FIRST = (8, 7, 5), (8, 7, 5)
BALANCE, FIXES = 4, 6


def place():
    w = lax.axis_index("wide")
    return w // (2 * NX), lax.rem(w // 2, NX), lax.rem(w, 2)


def wide(y, x, q):
    return {"wide": (y * NX + x) * 2 + q}


NEAR = 10


def item(axis, distance, other):
    if distance == 0:
        return other
    if distance == 2:
        return NEAR + "xy".index(axis) * 2 + other
    return 2 + "xy".index(axis) * 4 + (distance - 1) + other


ITEMS = 2 * (NX + NY - 1)


def neighbours():
    y, x, q = place()
    return {
        ("x", 1): wide(y, lax.rem(x + 1, NX), q),
        ("x", -1): wide(y, lax.rem(x + NX - 1, NX), q),
        ("y", 1): wide(lax.rem(y + 1, NY), x, q),
        ("y", -1): wide(lax.rem(y + NY - 1, NY), x, q),
        ("x", 2): wide(y, lax.rem(x + 2, NX), q),
        ("y", 2): wide(lax.rem(y + 2, NY), x, q),
        "core": wide(y, x, 1 - q),
    }


def courier(view, pieces, send, recv):
    near = neighbours()
    started = []

    def both(src, dst, piece, to, sem, origin=None):
        cut, at = pieces[piece]
        return pltpu.make_async_remote_copy(
            src_ref=view(src, cut) if origin is None else origin.at[cut],
            dst_ref=view(dst, cut),
            send_sem=send.at[sem],
            recv_sem=recv.at[dst, at],
            device_id=near[to],
            device_id_type=MESH,
        )

    def copy(src, dst, piece, to, origin=None):
        c = both(src, dst, piece, to, len(started), origin)
        c.start()
        started.append(c)

    def arrived(dst, piece):
        both(dst, dst, piece, "core", 0).wait_recv()

    def drain():
        for c in started:
            c.wait_send()

    return copy, arrived, drain


def gather_blocks(own, close, distant, send, recv):
    def view(k, cut):
        return close.at[(k,) + cut] if k < NEAR else distant.at[(k - NEAR,) + cut]

    copy, arrived, drain = courier(view, (((0,), 0), ((1,), 1)), send, recv)

    def start():
        for first in (0, 1):
            for a in "xy":
                copy(0, item(a, 3, 0), first, (a, 1), own)
                copy(0, item(a, 1, 0), 1 - first, (a, -1), own)
        for half in (0, 1):
            copy(0, 1, half, "core", own)

    def relay():
        for a in "xy":
            arrived(item(a, 3, 0), 0)
            copy(item(a, 3, 0), item(a, 2, 0), 0, (a, 1))
            arrived(item(a, 1, 0), 1)
            copy(item(a, 1, 0), item(a, 2, 0), 1, (a, -1))
        for a in "xy":
            copy(item(a, 3, 0), item(a, 3, 1), 0, "core")
            copy(item(a, 1, 0), item(a, 1, 1), 1, "core")

    def near():
        for a in "xy":
            arrived(item(a, 3, 0), 1)
            copy(item(a, 3, 0), item(a, 3, 1), 1, "core")
            arrived(item(a, 1, 0), 0)
            copy(item(a, 1, 0), item(a, 1, 1), 0, "core")
        for half in (0, 1):
            arrived(1, half)
            for a in "xy":
                arrived(item(a, 1, 1), half)
                arrived(item(a, 3, 1), half)

    def far():
        for half in (0, 1):
            for a in "xy":
                arrived(item(a, 2, 0), half)
                copy(item(a, 2, 0), item(a, 2, 1), half, "core")

    def finish():
        for half in (0, 1):
            for a in "xy":
                arrived(item(a, 2, 1), half)
        drain()

    return start, relay, near, far, finish


def exchange(buf, first, size, send, recv):
    cut = size // 2
    pieces = ((pl.ds(first, size),), 0), ((pl.ds(first, cut),), 0), ((pl.ds(first + cut, size - cut),), 1)
    copy, arrived, drain = courier(lambda k, cut: buf.at[(k,) + cut], pieces, send, recv)

    def start():
        for a in "xy":
            copy(0, item(a, 2, 0), 0, (a, 2))
        for a in "xy":
            copy(0, item(a, 3, 0), 0, (a, 1))
            copy(0, item(a, 1, 0), 0, (a, -1))
        copy(0, 1, 0, "core")

    def relay():
        for a in "xy":
            arrived(item(a, 3, 0), 0)
            copy(item(a, 3, 0), item(a, 3, 1), 0, "core")
            arrived(item(a, 1, 0), 0)
            copy(item(a, 1, 0), item(a, 1, 1), 0, "core")

    def far():
        for a in "xy":
            arrived(item(a, 2, 0), 0)
            copy(item(a, 2, 0), item(a, 2, 1), 0, "core")

    def finish():
        arrived(1, 0)
        for a in "xy":
            for d in (1, 3, 2):
                arrived(item(a, d, 1), 0)
        drain()

    return start, relay, far, finish


def encode(out, value):
    g = value.shape[0]
    rows = out.shape[1]
    halves = [value[:, :, :LANES], value[:, :, LANES:]]
    most = jnp.concatenate(
        [jnp.max(jnp.abs(h), axis=1) for h in halves] + [jnp.zeros((rows - 2 * g, LANES), jnp.float32)], axis=0
    )
    level = jnp.ceil(jnp.log2(jnp.maximum(most, 1e-30)) * STEP)
    out[2 * g] = level.astype(jnp.int32).astype(jnp.int16)
    inverse = jnp.exp2(level * (-1.0 / STEP)) * TOP
    for k in range(2):
        scaled = jnp.round(halves[k] * inverse[k * g : (k + 1) * g][:, None, :])
        out[k * g : (k + 1) * g] = scaled.astype(jnp.int32).astype(jnp.int16)


def scales(code):
    return jnp.exp2(code.astype(jnp.int32).astype(jnp.float32) * (1.0 / STEP)) * (1.0 / TOP)


def decode(ref):
    g = ref.shape[0] // 2
    scale = scales(ref[2 * g])
    tiles = ref[: 2 * g].astype(jnp.int32).astype(jnp.float32) * scale[: 2 * g][:, None, :]
    return jnp.concatenate([tiles[:g], tiles[g:]], axis=2)


def summed(value, axis):
    return jnp.sum(value, axis=axis, keepdims=True)


def balance(lo, hi, chosen):
    up = lax.broadcasted_iota(jnp.int32, (NODES, NODES), 0)
    across = lax.broadcasted_iota(jnp.int32, (NODES, NODES), 1)
    chip = lax.broadcasted_iota(jnp.int32, (NODES, lo.shape[1]), 0)
    is_lo = ((chip == lo) & chosen).astype(jnp.float32)
    is_hi = ((chip == hi) & chosen).astype(jnp.float32)
    lanes = (((1,), (1,)), ((), ()))
    count = lax.dot_general(is_lo, is_hi, lanes, preferred_element_type=jnp.float32)
    count += lax.dot_general(is_hi, is_lo, lanes, preferred_element_type=jnp.float32)
    same = up == across
    loops = jnp.where(same, count * 0.5, 0.0)
    count = jnp.where(same, 0.0, count)
    loops_up, loops_across = summed(loops, 1), summed(loops, 0)

    def loads(give):
        return summed(give, 1) + loops_up, summed(count - give, 0) + loops_across

    give = count * 0.5
    for _ in range(BALANCE):
        load_up, load_across = loads(give)
        give = jnp.clip(give - (load_up - load_across) * (1.0 / NODES), 0.0, count)
    give = jnp.where(up < across, jnp.floor(give + 0.5), count - jnp.floor(count - give + 0.5))
    tag_up, tag_across = up.astype(jnp.float32), across.astype(jnp.float32)
    for _ in range(FIXES):
        load_up, load_across = loads(give)
        full_up, full_across = load_up * 64.0 + tag_up, load_across * 64.0 + tag_across
        full = jnp.max(jnp.max(full_across, axis=1, keepdims=True), axis=0, keepdims=True)
        target = jnp.where((full_up == full) & (give > 0.0), full_across, 1e9)
        mirror = jnp.where((full_across == full) & (count - give > 0.0), full_up, 1e9)
        least = jnp.min(jnp.min(target, axis=1, keepdims=True), axis=0, keepdims=True)
        move = (full - least >= 128.0).astype(jnp.float32)
        give = give - jnp.where(target == least, move, 0.0) + jnp.where(mirror == least, move, 0.0)
    share = lax.dot_general(give, is_lo, (((0,), (0,)), ((), ())), preferred_element_type=jnp.float32)
    return summed(share * is_hi, 0)


def tables(pairs, turn):
    y, x, q = place()
    n = pairs.shape[1]
    up = lax.broadcasted_iota(jnp.int32, (n, n), 0)
    across = lax.broadcasted_iota(jnp.int32, (n, n), 1)
    same, before = up == across, up < across

    def column(v):
        return summed(jnp.where(same, v, 0), 1)

    def ranks(key):
        return summed(jnp.where((column(key) == key) & before, 1, 0), 0)

    r, c = pairs[0:1, :], pairs[1:2, :]
    yr, xr, yc, xc = r >> 3, (r >> 1) & 3, c >> 3, (c >> 1) & 3
    far_x, far_y = ((xr - xc) & 3) == 2, ((yr - yc) & 3) == 2
    middle_x, middle_y = far_x & (yr == yc), far_y & (xr == xc)
    late = (far_x | far_y) & jnp.logical_not(middle_x | middle_y)
    kind = late.astype(jnp.int32)
    one, two = yr * NX + xc, yc * NX + xr
    one = jnp.where(middle_x, yr * NX + ((xr + 1) & 3), jnp.where(middle_y, ((yr + 1) & 3) * NX + xr, one))
    two = jnp.where(middle_x, yr * NX + ((xr + 3) & 3), jnp.where(middle_y, ((yr + 3) & 3) * NX + xr, two))
    lo, hi = jnp.minimum(one, two), jnp.maximum(one, two)
    share = jnp.where(late, balance(lo, hi, late), balance(lo, hi, jnp.logical_not(late)))
    rank = ranks((lo * NODES + hi) * 2 + kind)
    node = jnp.where(rank.astype(jnp.float32) < share, lo, hi)
    rank = ranks(node * 2 + kind)
    node_up = column(node)
    ahead = summed(jnp.where((node_up == node) & (column(kind) == 0), 1, 0), 0)
    rank = jnp.where(late, jnp.maximum(ahead, 2 * HEAD) + rank, rank)
    most = jnp.broadcast_to(jnp.max(rank, axis=1, keepdims=True) + 1, (1, LANES))

    r, c, node, rank = column(r), column(c), node_up, column(rank)
    core, slot = rank & 1, (rank >> 1) - turn * TAIL
    inside = (slot >= jnp.where(turn > 0, HEAD, 0)) & (slot < SLOTS)
    lane = lax.broadcasted_iota(jnp.int32, (r.shape[0], LANES), 1)

    def seen(block_y, block_x, other):
        aside = block_y != y
        d = jnp.where(aside, block_y - y, block_x - x) & 3
        line = aside.astype(jnp.int32)
        return other + jnp.where(d == 0, 0, jnp.where(d == 2, NEAR + 2 * line, 1 + 4 * line + d))

    pick = (node == y * NX + x) & (core == q) & inside & (slot == lane)
    rows = summed(jnp.where(pick, seen(r >> 3, (r >> 1) & 3, (r & 1) ^ q), 0), 0)
    cols = summed(jnp.where(pick, seen(c >> 3, (c >> 1) & 3, (c & 1) ^ q), 0), 0)
    want = (r == (y * NX + x) * 2 + q) & inside & (c == lane)
    src = summed(jnp.where(want, seen(node >> 2, node & 3, core ^ q), 0), 0)
    at = summed(jnp.where(want, slot, 0), 0)
    live = summed(jnp.where(want, 1, 0), 0)
    rows, cols, src = [jnp.minimum(v, ITEMS - 1) for v in (rows, cols, src)]
    return rows, cols, src, jnp.minimum(at, SLOTS - 1), live, most


PARENTS = {
    "ring": {k: k - 1 for k in range(1, 9)},
    "skip": {8: 6, 7: 6, 6: 4, 5: 4, 4: 2, 3: 2, 2: 0, 1: 0},
    "mix": {8: 6, 7: 6, 6: 4, 5: 4, 4: 2, 3: 2, 2: 1, 1: 0},
}


def trees(group):
    pattern, longer = ROUTES[group]
    return [{k: p for k, p in PARENTS[pattern].items() if k < 8 or side == longer} for side in (0, 1)]


def kernel(
    nz, turn, pairs, factors, out, again_out, echo, close, distant, partial, z_out, z_in, parts, scale, table, table_s,
    listed, listed_sem, local, gsend, grecv, zsend, zrecv, xsend, xrecv,
):
    z = lax.axis_index("narrow")
    rows = close.shape[2]
    chunk = rows // nz
    forest = [trees(0)] * len(EARLY) + [trees(1)] * len(LATE)
    starts = [sum(STREAMS[:s]) for s in range(len(STREAMS))]

    def away(d):
        return {"narrow": lax.rem(z + d + nz, nz)}

    own = pltpu.make_async_copy(factors, close.at[0], local)
    own.start()
    listing = pltpu.make_async_copy(pairs, listed, listed_sem)
    listing.start()
    barrier = pltpu.get_barrier_semaphore()
    hops = sorted({sign * (k - p) for trees in forest for t in trees for k, p in t.items() for sign in (1, -1)})
    peers = list(neighbours().values()) + [away(d) for d in hops]
    for peer in peers:
        pl.semaphore_signal(barrier, inc=1, device_id=peer, device_id_type=MESH)
    pl.semaphore_wait(barrier, len(peers))

    start, relay, near, far, finish = gather_blocks(factors, close, distant, gsend, grecv)
    start()
    listing.wait()
    own.wait()
    for k, v in enumerate(tables(listed[...], turn[0])):
        table[k : k + 1, :] = v
    scalars = pltpu.make_async_copy(table, table_s, local)
    scalars.start()
    relay()
    scalars.wait()
    again_out[0] = jnp.where(table_s[5, 0] > 2 * (HEAD + (turn[0] + 1) * TAIL), 1, 0)
    echo[...] = listed[...]

    def tile(s, load):
        i, j = table_s[0, s], table_s[1, s]
        contract = (((1,), (1,)), ((), ()))
        partial[s] = sum(
            lax.dot_general(load(i, p), load(j, p), contract, preferred_element_type=jnp.float32) for p in (0, 1)
        )

    def load_close(i, p):
        return close[jnp.minimum(i, NEAR - 1), p]

    def load_any(i, p):
        return jnp.where(i < NEAR, load_close(i, p), distant[jnp.maximum(i - NEAR, 0), p])

    def span(stream):
        at = 2 * starts[stream] + stream
        return pl.ds(at, 2 * STREAMS[stream] + 1)

    def mine(dest, stream):
        at = pl.multiple_of(dest * chunk, chunk)
        return partial[pl.ds(starts[stream], STREAMS[stream]), pl.ds(at, chunk), :]

    def hop(side, k, stream):
        buf = side * (nz // 2) + k - 1
        return pltpu.make_async_remote_copy(
            src_ref=z_out.at[buf, span(stream)],
            dst_ref=z_in.at[buf, span(stream)],
            send_sem=zsend.at[buf, stream],
            recv_sem=zrecv.at[buf, stream],
            device_id=away((1, -1)[side] * (k - forest[stream][side][k])),
            device_id_type=MESH,
        )

    sent = []

    def gathered(side, k, stream, value):
        for child, parent in sorted(forest[stream][side].items(), reverse=True):
            if parent == k:
                hop(side, child, stream).wait_recv()
                value += decode(z_in.at[side * (nz // 2) + child - 1, span(stream)])
        return value

    def send(side, k, stream):
        dest = lax.rem(z + (1, -1)[side] * k + nz, nz)
        value = gathered(side, k, stream, mine(dest, stream))
        encode(z_out.at[side * (nz // 2) + k - 1, span(stream)], value)
        c = hop(side, k, stream)
        c.start()
        sent.append(c)

    def leg(ks, streams):
        for stream in streams:
            for k in ks:
                for side in (0, 1):
                    if k in forest[stream][side]:
                        send(side, k, stream)

    def make(streams, load):
        def one(s, _):
            tile(s, load)
            return 0

        for stream in streams:
            lax.fori_loop(starts[stream], starts[stream] + STREAMS[stream], one, 0)

    groups = (range(len(EARLY)), range(len(EARLY), len(STREAMS)))
    near()
    make(groups[0], load_close)
    leg(FIRST[0], groups[0])
    far()
    leg((6,), groups[0])
    finish()
    make(groups[1], load_any)
    leg(FIRST[1], groups[1])
    leg((3,), groups[0])
    for group, ks in STEPS[1:]:
        leg(ks, groups[group])
    swaps = []
    for stream, g in enumerate(STREAMS):
        value = mine(z, stream)
        for side in (1, 0):
            value = gathered(side, 0, stream, value)
        encode(parts.at[0, span(stream)], value)
        swaps.append(exchange(parts, 2 * starts[stream] + stream, 2 * g + 1, xsend.at[stream], xrecv.at[stream]))
        swaps[-1][0]()
    for swap in swaps:
        swap[1]()
    for swap in swaps:
        swap[2]()
    for swap in swaps:
        swap[3]()
    for k in range(ITEMS):
        for stream, g in enumerate(STREAMS):
            s = scales(parts[k, 2 * starts[stream] + stream + 2 * g])
            for j in range(g):
                scale[k * SLOTS + starts[stream] + j, 0:1, :] = s[j : j + 1]
                scale[k * SLOTS + starts[stream] + j, 1:2, :] = s[g + j : g + j + 1]
    nblk = out.shape[1] // rows
    for c in range(nblk):
        src, slot, live = table_s[2, c], table_s[3, c], table_s[4, c]
        first, step = slot, STREAMS[0]
        for stream in range(1, len(STREAMS)):
            later = slot >= starts[stream]
            first = jnp.where(later, slot + starts[stream] + stream, first)
            step = jnp.where(later, STREAMS[stream], step)
        s = scale[src * SLOTS + slot]
        for h in range(2):
            found = parts[src, first + h * step].astype(jnp.int32).astype(jnp.float32) * s[h : h + 1]
            out[:, c * rows + h * LANES : c * rows + (h + 1) * LANES] = jnp.where(live > 0, found, 0.0)
    for c in sent:
        c.wait_send()


def shards(factors, pairs):
    nz = lax.axis_size("narrow")
    two, rows, occ = factors.shape
    nblk = lax.axis_size("wide")
    chunk = rows // nz
    tiles = 2 * SLOTS + len(STREAMS)
    hops = (nz, len(STREAMS))
    pairs = pairs.T

    def run(pairs, turn):
        return pl.pallas_call(
            functools.partial(kernel, nz),
            out_shape=(
                jax.ShapeDtypeStruct((chunk, nblk * rows), jnp.float32),
                jax.ShapeDtypeStruct((1,), jnp.int32),
                jax.ShapeDtypeStruct(pairs.shape, jnp.int32),
            ),
            in_specs=[
                pl.BlockSpec(memory_space=pltpu.SMEM),
                pl.BlockSpec(memory_space=pl.ANY),
                pl.BlockSpec(memory_space=pl.ANY),
            ],
            out_specs=[
                pl.BlockSpec(memory_space=pltpu.VMEM),
                pl.BlockSpec(memory_space=pltpu.SMEM),
                pl.BlockSpec(memory_space=pltpu.VMEM),
            ],
            scratch_shapes=[
                pltpu.VMEM((NEAR, two, rows, occ), jnp.bfloat16),
                pltpu.VMEM((ITEMS - NEAR, two, rows, occ), jnp.bfloat16),
                pltpu.VMEM((SLOTS, rows, rows), jnp.float32),
                pltpu.VMEM((nz, tiles, chunk, LANES), jnp.int16),
                pltpu.VMEM((nz, tiles, chunk, LANES), jnp.int16),
                pltpu.VMEM((ITEMS, tiles, chunk, LANES), jnp.int16),
                pltpu.VMEM((ITEMS * SLOTS, 8, LANES), jnp.float32),
                pltpu.VMEM((8, LANES), jnp.int32),
                pltpu.SMEM((8, LANES), jnp.int32),
                pltpu.VMEM(pairs.shape, jnp.int32),
                pltpu.SemaphoreType.DMA,
                pltpu.SemaphoreType.DMA,
                pltpu.SemaphoreType.DMA((2 * ITEMS - 2,)),
                pltpu.SemaphoreType.DMA((ITEMS, 2)),
                pltpu.SemaphoreType.DMA(hops),
                pltpu.SemaphoreType.DMA(hops),
                pltpu.SemaphoreType.DMA((len(STREAMS), 15)),
                pltpu.SemaphoreType.DMA((len(STREAMS), ITEMS, 2)),
            ],
            compiler_params=pltpu.CompilerParams(
                collective_id=0, has_side_effects=True, vmem_limit_bytes=62 * 1024 * 1024
            ),
        )(turn, pairs, factors)

    out, more, pairs = run(pairs, jnp.zeros((1,), jnp.int32))

    def rest(pairs, out):
        def again(state):
            turn, out, _, pairs = state
            further, more, pairs = run(pairs, turn[None])
            return turn + 1, out + further, more, pairs

        state = (jnp.int32(1), out, jnp.ones((1,), jnp.int32), pairs)
        return lax.while_loop(lambda state: state[2][0] > 0, again, state)[1]

    return lax.switch(more[0], [lambda pairs, out: out, rest], pairs, out)


def solution(mesh):
    placed = (P("narrow", "wide", None), P())
    return jax.shard_map(
        shards, mesh=mesh, in_specs=placed, out_specs=P(("wide", "narrow"), None), check_vma=False
    )
```
